128 devices in a mesh: label: 32 (over z, y, x_lo), dp: 4 (over x_hi, core).
Axes of the slice: x: 4 (x_hi: 2, x_lo: 2; x = x_hi * 2 + x_lo), y: 4, z: 4, core: 2. Of those that a mesh axis runs over, the one named last changes fastest.
Arguments:
- queries: bfloat16 [16384, 1024], P(('label', 'dp')), may hold values from -6 to 6
- label_ids: int32 [16384, 8], P(('label', 'dp')), may hold values from 0 to 32767
- label_counts: int32 [16384], P(('label', 'dp')), may hold values from 1 to 8
- weights: bfloat16 [32768, 1024], P('label'), may hold values from -0.1875 to 0.1875
- encoder: bfloat16 [1024, 192], replicated, may hold values from -0.1875 to 0.1875
- decoder: bfloat16 [192, 1024], replicated, may hold values from -6 to 6
Outputs:
- query_grad: bfloat16 [16384, 1024], P(('label', 'dp'))
- weight_grad: bfloat16 [32768, 1024], P('label', 'dp')
The draws below stay inside these ranges and needn't reach their ends.
Inputs may be any that keep to these rules, and one draw needn't show every extreme that they name: `label_ids`: entries of a row past that row's count are ignored; a row may name a label more than once.
All inputs are finite; a program needn't handle non-finite values.
Results may differ from the reference program's by a relative error of at most 0.0033.
Values may be sent and summed in bfloat16 or wider, within the bound.
No kernel may reach another device: no remote copies, remote signals or barrier semaphores. Data moves between devices by JAX's collectives and lax.ppermute only.
A program may use at most 192 MiB of HBM per device.

```python
import math
import jax
import jax.numpy as jnp
import numpy as np
from jax import lax

D = 1024
R = 192
K = 8
TOK_DEV = 128
LAB_DEV = 1024
GROUP_ROWS = 4096
QUERIES = 16384
LABELS = 32768
N_LABEL = 32
N_DP = 4


def set_ends(drawn, stream_key, smallest, largest):
    longest = drawn.shape.index(max(drawn.shape))
    spots = []
    for shift in (0, 1):
        where = [jax.random.randint(jax.random.fold_in(stream_key, axis), (), 0, length) for axis, length in enumerate(drawn.shape)]
        where[longest] = (where[longest] + shift) % drawn.shape[longest]
        spots.append(tuple(where))
    return drawn.at[spots[0]].set(smallest).at[spots[1]].set(largest)


def level_of(key, extent, split, least, largest):
    loudness = 1.0
    for position, shards_of in split:
        steps = jax.random.uniform(jax.random.fold_in(jax.random.fold_in(key, 6), position), (shards_of,), jnp.float32, least / len(split), largest / len(split))
        loudness = loudness * jnp.repeat(jnp.exp(steps), extent[position] // shards_of).reshape((-1,) + (1,) * (len(extent) - 1 - position))
    return loudness


def rank_table(number_of, lean):
    weights = [(1 << 20) // math.isqrt(rank ** lean) + 1 for rank in range(1, number_of + 1)]
    deviation = 1 + sum(weights) // (1 << 30)
    return np.cumsum(np.array([max(1, weight // deviation) for weight in weights]))


def skewed_ids(own_key, extent, number_of, slope):
    grid = rank_table(number_of, slope)
    ticket = jax.random.randint(jax.random.fold_in(own_key, 1), extent, 0, int(grid[number_of - 1]))
    grade = jnp.searchsorted(jnp.asarray(grid, jnp.int32), ticket, side="right")
    return jax.random.permutation(jax.random.fold_in(own_key, 2), number_of)[grade].astype(jnp.int32)


def normal_values(key, shape, scale, bound, split=(), held_as=jnp.bfloat16):
    values = scale * jax.random.normal(key, shape, jnp.float32)
    if split:
        values = values * level_of(key, shape, split, -0.22, 0.18)
    return jnp.clip(values, -bound, bound).astype(held_as)


def setup_inputs(seed: int = 0) -> dict:
    seeds = jax.random.split(jax.random.key(seed), 7)
    return {
        "queries": normal_values(seeds[0], (QUERIES, D), 1.0, 6.0, ((0, 128),)),
        "label_ids": set_ends(skewed_ids(seeds[1], (QUERIES, K), LABELS, 2), jax.random.fold_in(seeds[1], 3), 0, LABELS - 1).astype(jnp.int32),
        "label_counts": set_ends(jax.random.randint(seeds[2], (QUERIES,), 1, K + 1), jax.random.fold_in(seeds[2], 1), 1, K).astype(jnp.int32),
        "weights": normal_values(seeds[3], (LABELS, D), D ** -0.5, 0.1875, ((0, 32),)),
        "encoder": normal_values(seeds[4], (D, R), D ** -0.5, 0.1875),
        "decoder": normal_values(seeds[5], (R, D), 1.0, 6.0),
    }


def shard_terms(rows, ids, counts, shard, offset, encoder, scale):
    logits = jnp.dot(rows, shard.T, preferred_element_type=jnp.float32)
    local = ids - offset
    live = jnp.arange(K, dtype=jnp.int32)[None, :] < counts[:, None]
    labels_here = jnp.arange(shard.shape[0], dtype=jnp.int32)
    hit = (local[:, :, None] == labels_here[None, None, :]) & live[:, :, None]
    target = jnp.any(hit, axis=1).astype(jnp.float32)
    grad = ((jax.nn.sigmoid(logits) - target) * scale).astype(jnp.bfloat16)
    partial_value = jnp.dot(grad, shard, preferred_element_type=jnp.float32)
    encoded = jnp.dot(partial_value, encoder.astype(jnp.float32), precision=lax.Precision.HIGHEST)
    wpart = jnp.dot(grad.T, rows, preferred_element_type=jnp.float32)
    return encoded, wpart


def regroup(array):
    tail = array.shape[1:]
    blocks = array.reshape((N_LABEL, N_DP, TOK_DEV) + tail)
    blocks = jnp.swapaxes(blocks, 0, 1)
    return blocks.reshape((N_DP, GROUP_ROWS) + tail)


def reference(queries, label_ids, label_counts, weights, encoder, decoder):
    scale = float(QUERIES) ** -0.5
    rows = regroup(queries)
    ids = regroup(label_ids)
    counts = regroup(label_counts)

    def one_shard(carry, index):
        offset = (index * LAB_DEV).astype(jnp.int32)
        shard = lax.dynamic_slice_in_dim(weights, offset, LAB_DEV, 0)
        encoded, wparts = jax.vmap(lambda r, i, c: shard_terms(r, i, c, shard, offset, encoder, scale))(rows, ids, counts)
        wgrad = jnp.sum(wparts, axis=0).astype(jnp.bfloat16)
        return carry + encoded, wgrad

    start = jnp.zeros((N_DP, GROUP_ROWS, R), jnp.float32)
    encoded, wgrads = lax.scan(one_shard, start, jnp.arange(N_LABEL, dtype=jnp.int32))
    blocks = encoded.reshape(N_DP, N_LABEL, TOK_DEV, R)
    blocks = jnp.swapaxes(blocks, 0, 1).reshape(QUERIES, R)
    query_grad = jnp.dot(blocks, decoder.astype(jnp.float32), precision=lax.Precision.HIGHEST).astype(jnp.bfloat16)
    weight_grad = wgrads.reshape(LABELS, D)
    return query_grad, weight_grad
```

```python
import functools
import itertools

import jax
import jax.numpy as jnp
from jax import lax
from jax.experimental import pallas as pl
from jax.experimental.pallas import tpu as pltpu
from jax.sharding import Mesh, PartitionSpec as P

AXES = ("z", "y", "xl", "xh", "core")
BF16, F32, I32 = jnp.bfloat16, jnp.float32, jnp.int32
TAIL = 16
BLOCK = 256


def pairs(target):
    flat = lambda z, y, x, c: (((z % 4 * 4 + y % 4) * 2 + x % 2) * 2 + x % 4 // 2) * 2 + c
    places = itertools.product(range(4), range(4), range(4), range(2))
    return [(flat(*at), flat(*target(*at))) for at in places if target(*at) is not None]


def move(array, target):
    return lax.ppermute(array, AXES, pairs(target))


def hop(phase, step):
    return lambda z, y, x, c: (z + step, y, x, c) if c == phase else (z, y + step, x, c)


def to_sibling(z, y, x, c):
    return z, y, x, 1 - c


def weights_from(step):
    return lambda z, y, x, c: (z, y, x + step, c) if c == x % 2 else (z, y, x, 1 - c)


def encode_kernel(w_ref, enc_ref, out_ref):
    we = lax.dot_general(
        enc_ref[...], w_ref[...], (((1,), (1,)), ((), ())), preferred_element_type=F32
    )
    high = we.astype(BF16)
    out_ref[:192, :] = high
    out_ref[192:, :] = (we - high.astype(F32)).astype(BF16)


def target_bits(tail, block, base, step):
    digits = tail[2 * block : 2 * block + 2, :]
    local = (digits[0:1] * 256 + digits[1:2]) - base
    word = jnp.where((local >> 8) == step, jnp.left_shift(1, (local >> 3) & 31), 0)
    low = local & 7
    row = lax.broadcasted_iota(I32, (8, 128), 0)
    bits = jnp.zeros((8, 128), I32)
    for slot in range(8):
        lanes = slice(slot * 128, (slot + 1) * 128)
        here = jnp.broadcast_to(low[:, lanes], (8, 128)) == row
        bits = bits | jnp.where(here, jnp.broadcast_to(word[:, lanes], (8, 128)), 0)
    return bits


def chunk_kernel(pieces, n_q, enc_widths, first, last, scale, *refs):
    place = refs[0]
    q_refs = refs[1 : 1 + n_q]
    w_ref, wet_ref = refs[1 + n_q : 3 + n_q]
    rest = refs[3 + n_q :]
    if not first:
        total_ref, rest = rest[0], rest[1:]
    enc_refs, outs = rest[: len(enc_widths)], rest[len(enc_widths) :]
    step = pl.program_id(0)
    base = place[0]
    w = w_ref[...]
    wet = wet_ref[...]

    @pl.when(step == 0)
    def _():
        for ref in enc_refs:
            ref[...] = jnp.zeros_like(ref)

    group = lax.broadcasted_iota(I32, (BLOCK // 8, 1, 1), 0)
    total = None if first else total_ref[...]
    tails = {}
    for q, rows, t, offset, block, out, column in pieces:
        if t not in tails:
            tails[t] = q_refs[t][offset : offset + TAIL, :].astype(F32).astype(I32)
        queries = q_refs[q][:rows, :]
        logits = lax.dot_general(
            w, queries, (((1,), (1,)), ((), ())), preferred_element_type=F32
        )
        bits = jnp.concatenate(
            [target_bits(tails[t], block + b, base, step) for b in range(rows // 128)], axis=1
        )
        hit = (bits[None] >> group) & 1
        target = hit.reshape(BLOCK, rows).astype(F32)
        grad = ((jax.nn.sigmoid(logits) - target) * scale).astype(BF16)
        encoded = jnp.dot(wet, grad, preferred_element_type=F32)
        enc_refs[out][:, column : column + rows] += encoded[:192] + encoded[192:]
        part = jnp.dot(grad, queries, preferred_element_type=F32)
        total = part if total is None else total + part
    if last:
        left, right = total[:, :512], total[:, 512:]
        swap = place[1] == 0
        outs[0][...] = jnp.where(swap, left, right).astype(BF16)
        other = jnp.where(swap, right, left)
        outs[1][...] = other.astype(BF16)
        outs[2][...] = other
    else:
        outs[0][...] = total


def chunk(place, q_bufs, pieces, w, wet, total, enc_widths, last, scale):
    labels, width = w.shape
    first = total is None
    whole = lambda a: pl.BlockSpec(a.shape, lambda i: (0,) * a.ndim)
    rows = lambda n: pl.BlockSpec((BLOCK, n), lambda i: (i, 0))
    in_specs = [pl.BlockSpec(memory_space=pltpu.SMEM)]
    in_specs += [whole(a) for a in q_bufs]
    in_specs += [rows(width), pl.BlockSpec((2 * 192, BLOCK), lambda i: (0, i))]
    args = [place, *q_bufs, w, wet]
    if not first:
        in_specs.append(rows(width))
        args.append(total)
    shapes = [jax.ShapeDtypeStruct((192, n), F32) for n in enc_widths]
    out_specs = [whole(s) for s in shapes]
    if last:
        shapes += [jax.ShapeDtypeStruct((labels, 512), d) for d in (BF16, BF16, F32)]
        out_specs += [rows(512)] * 3
    else:
        shapes.append(jax.ShapeDtypeStruct((labels, width), F32))
        out_specs.append(rows(width))
    n = sum(p[1] for p in pieces)
    return pl.pallas_call(
        functools.partial(chunk_kernel, pieces, len(q_bufs), enc_widths, first, last, scale),
        grid=(labels // BLOCK,),
        in_specs=in_specs,
        out_specs=out_specs,
        out_shape=shapes,
        compiler_params=pltpu.CompilerParams(vmem_limit_bytes=40 * 2**20),
        cost_estimate=pl.CostEstimate(
            flops=2 * n * labels * (2 * width + 384), bytes_accessed=8 * 2**20, transcendentals=0
        ),
        name="chunk",
    )(*args)


def pack_kernel(index_ref, *refs):
    own, sib, out = refs[:4], refs[4:8], refs[8]
    for part in range(4):
        for block in range(4):
            lanes = slice(block * 128, block * 128 + 128)
            value = own[part][:, lanes] + sib[part][:, lanes]
            out[index_ref[part * 4 + block]] = value.astype(BF16)


def decode_kernel(parts_ref, dec_ref, out_ref):
    total = parts_ref[0].astype(F32)
    for i in range(1, 16):
        total += parts_ref[i].astype(F32)
    dec = dec_ref[...]
    rest, result = total, None
    for _ in range(3):
        digit = rest.astype(BF16)
        rest = rest - digit.astype(F32)
        part = lax.dot_general(digit, dec, (((0,), (0,)), ((), ())), preferred_element_type=F32)
        result = part if result is None else result + part
    out_ref[...] = result.astype(BF16)


def join_kernel(flag_ref, own_ref, a_ref, b_ref, c_ref, mine_ref, sib_ref):
    total = own_ref[...] + a_ref[...].astype(F32) + b_ref[...].astype(F32) + c_ref[...].astype(F32)
    total = total.astype(BF16)
    left, right = total[:, :256], total[:, 256:]
    first = flag_ref[0] == 0
    mine_ref[...] = jnp.where(first, left, right)
    sib_ref[...] = jnp.where(first, right, left)


def shards(queries, label_ids, label_counts, weights, encoder, decoder):
    z, y, xl, xh, core = (lax.axis_index(a) for a in AXES)
    x = 2 * xh + xl
    scale = float(queries.shape[0] * 128) ** (-0.5)
    labels = weights.shape[0]

    slot = lax.broadcasted_iota(I32, (8, 128), 0)
    ids = jnp.where(slot < label_counts[None, :], label_ids.T, 255 * 256).reshape(1, 1024)
    tail = jnp.concatenate([ids >> 8, ids & 255, jnp.zeros((TAIL - 2, 1024), I32)], axis=0)
    own = jnp.concatenate([queries, tail.astype(BF16)], axis=0)

    back, ahead = move(own, hop(0, 1)), move(own, hop(0, -1))
    w = jnp.concatenate(
        [move(weights[: labels // 2], weights_from(1)), move(weights[labels // 2 :], weights_from(-1))], axis=0
    )
    far0, far1 = move(back[:64], hop(0, 1)), move(ahead[64:], hop(0, -1))
    row = jnp.concatenate(
        [own[:128], back[:128], ahead[:128], far0, far1[:64]]
        + [own[128:130], back[128:130], ahead[128:130], far1[64:66], own[136:144]],
        axis=0,
    )
    row_back, row_ahead = move(row, hop(1, 1)), move(row, hop(1, -1))
    row_far0, row_far1 = move(row_back[:256], hop(1, 1)), move(row_ahead[256:], hop(1, -1))

    shard = (z * 4 + y) * 2 + core
    away = jnp.where(core == xl, 1 - xh, (x + 1) % 4 // 2)
    place = jnp.stack([shard * labels, away]).astype(I32)
    wet = pl.pallas_call(
        encode_kernel, out_shape=jax.ShapeDtypeStruct((384, labels), BF16), name="encode"
    )(w, encoder.T)

    whole = lambda q, out, column: (q, 512, q, 512, 0, out, column)
    enc_a, enc_sa, total = chunk(
        place, [row, move(row, to_sibling)], [whole(0, 0, 0), whole(1, 1, 0)],
        w, wet, None, (512, 512), False, scale,
    )
    enc_b, total = chunk(
        place, [row_back, row_ahead], [whole(0, 0, 0), whole(1, 0, 512)],
        w, wet, total, (1024,), False, scale,
    )
    enc_sb, total = chunk(
        place, [move(row_back, to_sibling), move(row_ahead, to_sibling)], [whole(0, 0, 0), whole(1, 0, 512)],
        w, wet, total, (1024,), False, scale,
    )
    half = lambda q, t, block, out: (q, 256, t, 256, block, out, block * 128)
    enc_c, enc_sc, out_a, out_b, kept = chunk(
        place, [row_far0, row_far1, move(row_far0, to_sibling), move(row_far1, to_sibling)],
        [half(0, 1, 0, 0), half(1, 1, 2, 0), half(2, 3, 0, 1), half(3, 3, 2, 1)],
        w, wet, total, (512, 512), True, scale,
    )

    other = lambda step: lambda z, y, x, c: (z, y, x + step, c) if c != x % 2 else None
    same = lambda z, y, x, c: (z, y, x + 2, c) if c == x % 2 else None
    got = [move(out_a, other(1)), move(out_b, other(-1)), move(out_a, same)]

    got_a, got_b, got_c = move(enc_sa, to_sibling), move(enc_sb, to_sibling), move(enc_sc, to_sibling)
    shift = jnp.array([0, 3, 1, 2], I32)
    first, second = jnp.where(core == 0, z, y), jnp.where(core == 0, y, z)
    first, second = (first + shift[None, :]) % 4, (second + shift[:, None]) % 4
    index = jnp.where(core == 0, first * 4 + second, second * 4 + first).reshape(16).astype(I32)
    vmem = pl.BlockSpec(memory_space=pltpu.VMEM)
    smem = pl.BlockSpec(memory_space=pltpu.SMEM)
    part = lambda j: pl.BlockSpec((192, 512), lambda i: (0, j))
    packed = pl.pallas_call(
        pack_kernel,
        grid=(1,),
        in_specs=[smem, part(0), part(0), part(1), part(0), part(0), part(0), part(1), part(0)],
        out_specs=pl.BlockSpec((16, 192, 128), lambda i: (0, 0, 0)),
        out_shape=jax.ShapeDtypeStruct((16, 192, 128), BF16),
        name="pack",
    )(index, enc_a, enc_b, enc_b, enc_c, got_a, got_b, got_b, got_c)
    parts = lax.all_to_all(packed, ("z", "y"), split_axis=0, concat_axis=0, tiled=True)
    query_grad = pl.pallas_call(
        decode_kernel, out_shape=jax.ShapeDtypeStruct((128, 1024), BF16), name="decode"
    )(parts, decoder)

    wide = pl.BlockSpec((256, 512), lambda i: (i, 0))
    narrow = pl.BlockSpec((256, 256), lambda i: (i, 0))
    mine, sib = pl.pallas_call(
        join_kernel,
        grid=(labels // 256,),
        in_specs=[smem, wide, wide, wide, wide],
        out_specs=[narrow, narrow],
        out_shape=[jax.ShapeDtypeStruct((labels, 256), BF16)] * 2,
        name="join",
    )(core.astype(I32).reshape(1), kept, *got)
    sib = move(sib, lambda z, y, x, c: (z, y, x, 1 - c) if c == x % 2 else None)
    weight_grad = jnp.where(core == xl, mine, sib)
    return query_grad, weight_grad


def solution(mesh):
    fine = Mesh(mesh.devices.reshape(4, 4, 2, 2, 2), AXES)
    label, dp = AXES[:3], AXES[3:]
    return jax.shard_map(
        shards,
        mesh=fine,
        in_specs=(P(AXES, None), P(AXES, None), P(AXES), P(label, None), P(), P()),
        out_specs=(P(AXES, None), P(label, dp)),
        check_vma=False,
    )
```

```python
import functools
import itertools

import jax
import jax.numpy as jnp
from jax import lax
from jax.experimental import pallas as pl
from jax.experimental.pallas import tpu as pltpu
from jax.sharding import Mesh, PartitionSpec as P

AXES = ("z", "y", "xl", "xh", "core")
BF16, F32, I32 = jnp.bfloat16, jnp.float32, jnp.int32
TAIL = 16
HALF = 512
VMEM_LIMIT = 16 * 2**20
OFFSETS = (0, 3, 1, 2)


def pairs(target):
    flat = lambda z, y, x, c: (((z % 4 * 4 + y % 4) * 2 + x % 2) * 2 + x % 4 // 2) * 2 + c
    places = itertools.product(range(4), range(4), range(4), range(2))
    return [(flat(*at), flat(*target(*at))) for at in places if target(*at) is not None]


def move(array, target):
    return lax.ppermute(array, AXES, pairs(target))


def hop(phase, step):
    return lambda z, y, x, c: (z + step, y, x, c) if c == phase else (z, y + step, x, c)


def to_sibling(z, y, x, c):
    return z, y, x, 1 - c


def to_user(z, y, x, c):
    return (z, y, x ^ 1, c) if c == x % 2 else (z, y, x, 1 - c)


def rows_kernel(own_ref, back_ref, ahead_ref, far_ref, low_ref, high_ref):
    low_ref[:128, :] = own_ref[:128, :]
    low_ref[128:, :] = back_ref[:128, :]
    high_ref[:128, :] = ahead_ref[:128, :]
    high_ref[128:256, :] = far_ref[:128, :]
    refs = (own_ref, back_ref, ahead_ref, far_ref)
    row = lax.broadcasted_iota(I32, (TAIL, 1024), 0)
    tail = jnp.zeros((TAIL, 1024), F32)
    for i, ref in enumerate(refs):
        ids = ref[128:144, :].astype(F32)
        for digit in range(2):
            tail = jnp.where(row == 2 * i + digit, ids[digit : digit + 1, :], tail)
    high_ref[256:, :] = tail.astype(BF16)


def encode(w_ref, enc_ref, wet_ref):
    we = lax.dot_general(
        enc_ref[...], w_ref[...], (((1,), (1,)), ((), ())), preferred_element_type=F32
    )
    high = we.astype(BF16)
    wet_ref[:192, :] = high
    wet_ref[192:, :] = (we - high.astype(F32)).astype(BF16)


def target_bits(tail, block, base):
    digits = tail[2 * block : 2 * block + 2, :]
    local = (digits[0:1] * 256 + digits[1:2]) - base
    low, bit = local & 7, jnp.left_shift(1, (local >> 3) & 31)
    words = [jnp.where((local >> 8) == w, bit, 0) for w in range(4)]
    row = lax.broadcasted_iota(I32, (8, 128), 0)
    bits = [jnp.zeros((8, 128), I32)] * 4
    for slot in range(8):
        lanes = slice(slot * 128, (slot + 1) * 128)
        here = jnp.broadcast_to(low[:, lanes], (8, 128)) == row
        for w in range(4):
            word = jnp.broadcast_to(words[w][:, lanes], (8, 128))
            bits[w] = bits[w] | jnp.where(here, word, 0)
    return bits


def quarters(x, core):
    keeps = core == lax.rem(x, 2)
    half, next_half = x // 2, lax.rem(x + 1, 4) // 2
    away = jnp.where(keeps, 1 - half, next_half)
    column = jnp.where(keeps, 1 - core, core)
    return 2 * away + column, 2 * (1 - away) + core, 2 * away + 1 - column, 2 * (1 - away) + 1 - core


def chunk_kernel(enc_at, first, last, scale, *refs):
    n = len(enc_at)
    place, q_refs, refs = refs[0], refs[1 : 1 + 2 * n], refs[1 + 2 * n :]
    z, y, x, core = (place[i] for i in range(4))
    base = ((z * 4 + y) * 2 + core) * 2 * HALF
    w_ref, enc_ref, refs = refs[0], refs[1], refs[2:]
    if not first:
        total_ref, refs = refs[0], refs[1:]
    outs, (q_all, grads, bits) = refs[:-3], refs[-3:]
    n_enc = 1 + max(out for out, _ in enc_at)
    encs, outs = outs[:n_enc], outs[n_enc:]
    if first:
        wet_ref, outs = outs[0], outs[1:]
        encode(w_ref, enc_ref, wet_ref)
    else:
        wet_ref = enc_ref
    for i in range(n):
        low, high = q_refs[2 * i : 2 * i + 2]
        q_all[512 * i : 512 * i + 256, :] = low[...]
        q_all[512 * i + 256 : 512 * i + 512, :] = high[:256, :]
        tail = high[256:272, :].astype(F32).astype(I32)
        for b in range(4):
            lanes = slice(512 * i + 128 * b, 512 * i + 128 * b + 128)
            for w, word in enumerate(target_bits(tail, b, base)):
                bits[w, :, lanes] = word
    group = lax.broadcasted_iota(I32, (32, 1, 1), 0)
    for i in range(2):
        rows = slice(i * HALF, (i + 1) * HALF)
        for j in range(n):
            lanes = slice(512 * j, 512 * j + 512)
            logits = lax.dot_general(
                w_ref[rows, :], q_all[lanes, :], (((1,), (1,)), ((), ())), preferred_element_type=F32
            )
            for w in range(2):
                hit = (bits[2 * i + w, :, lanes][None] >> group) & 1
                target = hit.reshape(256, 512).astype(F32)
                some = jax.nn.sigmoid(logits[w * 256 : w * 256 + 256]) - target
                grads[i * HALF + w * 256 : i * HALF + w * 256 + 256, lanes] = (some * scale).astype(BF16)
        if not last:
            part = jnp.dot(grads[rows, :], q_all[...], preferred_element_type=F32)
            for c in range(4):
                columns = slice(256 * c, 256 * c + 256)
                old = 0.0 if first else total_ref[c, rows, :]
                outs[0][c, rows, :] = old + part[:, columns]
    encoded = jnp.dot(wet_ref[...], grads[...], preferred_element_type=F32)
    encoded = encoded[:192] + encoded[192:]
    for i, (out, column) in enumerate(enc_at):
        encs[out][:, column : column + 512] = encoded[:, 512 * i : 512 * i + 512]
    if last:
        for o, c in enumerate(quarters(x, core)):
            columns = q_all[:, pl.ds(pl.multiple_of(c * 256, 256), 256)]
            whole = total_ref[c] + jnp.dot(grads[...], columns, preferred_element_type=F32)
            outs[o][...] = whole.astype(BF16)
            if o % 2:
                outs[4 + o // 2][...] = whole


def chunk(place, q_bufs, enc_at, w, enc, total, last, scale):
    first = total is None
    vmem = pl.BlockSpec(memory_space=pltpu.VMEM)
    widths = [0] * (1 + max(out for out, _ in enc_at))
    for out, column in enc_at:
        widths[out] = max(widths[out], column + 512)
    args = [place, *q_bufs, w, enc] + ([] if first else [total])
    labels = 2 * HALF
    shapes = [jax.ShapeDtypeStruct((192, n), F32) for n in widths]
    if first:
        shapes.append(jax.ShapeDtypeStruct((384, labels), BF16))
    if last:
        shapes += [jax.ShapeDtypeStruct((labels, 256), d) for d in (BF16,) * 4 + (F32,) * 2]
    else:
        shapes.append(jax.ShapeDtypeStruct((4, labels, 256), F32))
    n = 512 * len(enc_at)
    return pl.pallas_call(
        functools.partial(chunk_kernel, enc_at, first, last, scale),
        in_specs=[pl.BlockSpec(memory_space=pltpu.SMEM)] + [vmem] * (len(args) - 1),
        out_specs=[vmem] * len(shapes),
        out_shape=shapes,
        scratch_shapes=[
            pltpu.VMEM((n, 1024), BF16), pltpu.VMEM((labels, n), BF16), pltpu.VMEM((4, 8, n), I32)
        ],
        input_output_aliases={} if first or last else {len(args) - 1: len(shapes) - 1},
        compiler_params=pltpu.CompilerParams(vmem_limit_bytes=VMEM_LIMIT),
        cost_estimate=pl.CostEstimate(
            flops=2 * n * labels * (2 * 1024 + 384), bytes_accessed=2**20, transcendentals=0
        ),
        name="chunk",
    )(*args)


def pack_kernel(place, *refs):
    own, sib, out = refs[:3], refs[3:6], refs[6]
    z, y, core = place[0], place[1], place[3]
    first, second = jnp.where(core == 0, z, y), jnp.where(core == 0, y, z)
    at = [(i, j) for i in OFFSETS for j in OFFSETS]
    for a, b in zip(own, sib):
        value = (a[...] + b[...]).astype(BF16)
        for block in range(value.shape[1] // 128):
            i, j = at.pop(0)
            j, i = lax.rem(first + j, 4), lax.rem(second + i, 4)
            out[jnp.where(core == 0, j * 4 + i, i * 4 + j)] = value[:, block * 128 : block * 128 + 128]


def decode_kernel(parts_ref, dec_ref, out_ref):
    total = parts_ref[0].astype(F32)
    for i in range(1, 16):
        total += parts_ref[i].astype(F32)
    dec = dec_ref[...]
    rest, result = total, None
    for _ in range(3):
        digit = rest.astype(BF16)
        rest = rest - digit.astype(F32)
        part = lax.dot_general(digit, dec, (((0,), (0,)), ((), ())), preferred_element_type=F32)
        result = part if result is None else result + part
    out_ref[...] = result.astype(BF16)


def join_kernel(place, own_ref, *refs):
    total = jnp.where(place[3] == lax.rem(place[2], 2), own_ref[...], 0.0)
    for ref in refs[:-1]:
        total += ref[...].astype(F32)
    refs[-1][...] = total.astype(BF16)


def kernel(body, out, *args, name, flops=10**6):
    place = lambda a: pltpu.SMEM if a.dtype == I32 else pltpu.VMEM
    one = not isinstance(out[0][0], tuple)
    shapes = [jax.ShapeDtypeStruct(*o) for o in ([out] if one else out)]
    result = pl.pallas_call(
        body,
        in_specs=[pl.BlockSpec(memory_space=place(a)) for a in args],
        out_specs=[pl.BlockSpec(memory_space=pltpu.VMEM)] * len(shapes),
        out_shape=shapes,
        compiler_params=pltpu.CompilerParams(vmem_limit_bytes=VMEM_LIMIT),
        cost_estimate=pl.CostEstimate(flops=flops, bytes_accessed=2**10, transcendentals=0),
        name=name,
    )(*args)
    return result[0] if one else result


def shards(queries, label_ids, label_counts, weights, encoder, decoder):
    z, y, xl, xh, core = (lax.axis_index(a) for a in AXES)
    scale = float(queries.shape[0] * 128) ** (-0.5)

    slot = lax.broadcasted_iota(I32, (8, 128), 0)
    ids = jnp.where(slot < label_counts[None, :], label_ids.T, 255 * 256).reshape(1, 1024)
    tail = jnp.concatenate([ids >> 8, ids & 255, jnp.zeros((TAIL - 2, 1024), I32)], axis=0)
    own = jnp.concatenate([queries, tail.astype(BF16)], axis=0)

    place = jnp.stack([z, y, 2 * xh + xl, core]).astype(I32)
    w = move(weights, to_user)
    back, ahead, far = (move(own, hop(0, step)) for step in (1, -1, 2))
    low, high = kernel(
        rows_kernel, (((256, 1024), BF16), ((256 + TAIL, 1024), BF16)), own, back, ahead, far, name="rows"
    )
    low_back, high_ahead = move(low, hop(1, 1)), move(high, hop(1, -1))
    high_back, low_ahead = move(high, hop(1, 1)), move(low, hop(1, -1))
    low_far, high_far = move(low_back, hop(1, 1)), move(high_ahead, hop(1, -1))
    rows, backs, aheads, fars = [low, high], [low_back, high_back], [low_ahead, high_ahead], [low_far, high_far]
    sibling = lambda bufs: [move(b, to_sibling) for b in bufs]

    apart, joined = ((0, 0), (1, 0)), ((0, 0), (0, 512))
    enc_a, enc_sa, wet, total = chunk(place, rows + sibling(rows), apart, w, encoder.T, None, False, scale)
    enc_b, total = chunk(place, backs + aheads, joined, w, wet, total, False, scale)
    enc_sb, total = chunk(place, sibling(backs) + sibling(aheads), joined, w, wet, total, False, scale)
    enc_c, enc_sc, out_0, out_1, out_2, out_3, kept, sib = chunk(
        place, fars + sibling(fars), apart, w, wet, total, True, scale
    )

    pick = lambda same, other: lambda z, y, x, c: same(z, y, x, c) if c == x % 2 else other(z, y, x, c)
    none = lambda z, y, x, c: None
    got = [
        move(out_0, pick(lambda z, y, x, c: (z, y, x + 2, 1 - c), lambda z, y, x, c: (z, y, x + 1, c))),
        move(out_1, pick(none, lambda z, y, x, c: (z, y, x - 1, c))),
        move(out_2, pick(lambda z, y, x, c: (z, y, x + 2, c), lambda z, y, x, c: (z, y, x + 1, 1 - c))),
        move(out_3, pick(none, lambda z, y, x, c: (z, y, x - 1, 1 - c))),
        move(sib, pick(to_sibling, none)),
    ]

    packed = kernel(
        pack_kernel, ((16, 192, 128), BF16), place, enc_a, enc_b, enc_c, *sibling([enc_sa, enc_sb, enc_sc]), name="pack"
    )
    parts = lax.all_to_all(packed, ("z", "y"), split_axis=0, concat_axis=0, tiled=True)
    query_grad = kernel(decode_kernel, ((128, 1024), BF16), parts, decoder, name="decode")
    weight_grad = kernel(join_kernel, ((2 * HALF, 256), BF16), place, kept, *got, name="join", flops=10**11)
    return query_grad, weight_grad


def solution(mesh):
    fine = Mesh(mesh.devices.reshape(4, 4, 2, 2, 2), AXES)
    label, dp = AXES[:3], AXES[3:]
    return jax.shard_map(
        shards,
        mesh=fine,
        in_specs=(P(AXES, None), P(AXES, None), P(AXES), P(label, None), P(), P()),
        out_specs=(P(AXES, None), P(label, dp)),
        check_vma=False,
    )
```

```python
import functools
import itertools

import jax
import jax.numpy as jnp
from jax import lax
from jax.experimental import pallas as pl
from jax.experimental.pallas import tpu as pltpu
from jax.sharding import Mesh, PartitionSpec as P

AXES = ("z", "y", "xl", "xh", "core")
BF16, F32, I32 = jnp.bfloat16, jnp.float32, jnp.int32
TAIL = 16
HALF = 512
VMEM_LIMIT = 16 * 2**20
OFFSETS = (0, 3, 1, 2)


def pairs(target):
    flat = lambda z, y, x, c: (((z % 4 * 4 + y % 4) * 2 + x % 2) * 2 + x % 4 // 2) * 2 + c
    places = itertools.product(range(4), range(4), range(4), range(2))
    return [(flat(*at), flat(*target(*at))) for at in places if target(*at) is not None]


def move(array, target):
    return lax.ppermute(array, AXES, pairs(target))


def hop(phase, step):
    return lambda z, y, x, c: (z + step, y, x, c) if c == phase else (z, y + step, x, c)


def to_sibling(z, y, x, c):
    return z, y, x, 1 - c


def to_user(z, y, x, c):
    return (z, y, x ^ 1, c) if c == x % 2 else (z, y, x, 1 - c)


def row_kernel(place, own_ref, back_ref, ahead_ref, far_ref, row_ref):
    refs = (own_ref, back_ref, ahead_ref, far_ref)
    for i, ref in enumerate(refs):
        row_ref[i * 128 : i * 128 + 128, :] = ref[:128, :]
    row = lax.broadcasted_iota(I32, (TAIL, 1024), 0)
    tail = jnp.zeros((TAIL, 1024), F32)
    for i, ref in enumerate(refs):
        ids = ref[128:144, :].astype(F32)
        for digit in range(2):
            tail = jnp.where(row == 2 * i + digit, ids[digit : digit + 1, :], tail)
    row_ref[512:, :] = tail.astype(BF16)


def halves_kernel(back_ref, ahead_ref, low_ref, high_ref):
    low_ref[...] = back_ref[:256, :]
    high_ref[...] = ahead_ref[256:, :]


def encode(w_ref, enc_ref, wet_ref):
    we = lax.dot_general(
        enc_ref[...], w_ref[...], (((1,), (1,)), ((), ())), preferred_element_type=F32
    )
    high = we.astype(BF16)
    wet_ref[:192, :] = high
    wet_ref[192:, :] = (we - high.astype(F32)).astype(BF16)


def target_bits(tail, block, base):
    digits = tail[2 * block : 2 * block + 2, :]
    local = (digits[0:1] * 256 + digits[1:2]) - base
    low, bit = local & 7, jnp.left_shift(1, (local >> 3) & 31)
    words = [jnp.where((local >> 8) == w, bit, 0) for w in range(4)]
    row = lax.broadcasted_iota(I32, (8, 128), 0)
    bits = [jnp.zeros((8, 128), I32)] * 4
    for slot in range(8):
        lanes = slice(slot * 128, (slot + 1) * 128)
        here = jnp.broadcast_to(low[:, lanes], (8, 128)) == row
        for w in range(4):
            word = jnp.broadcast_to(words[w][:, lanes], (8, 128))
            bits[w] = bits[w] | jnp.where(here, word, 0)
    return bits


def quarters(x, core):
    keeps = core == lax.rem(x, 2)
    half, next_half = x // 2, lax.rem(x + 1, 4) // 2
    away = jnp.where(keeps, 1 - half, next_half)
    column = jnp.where(keeps, 1 - core, core)
    return 2 * away + column, 2 * (1 - away) + column, 2 * away + 1 - column, 2 * (1 - away) + 1 - column


def chunk_kernel(parts, enc_at, first, last, scale, *refs):
    n = len(enc_at)
    n_q = sum(parts)
    place, q_refs, refs = refs[0], refs[1 : 1 + n_q], refs[1 + n_q :]
    z, y, x, core = (place[i] for i in range(4))
    base = ((z * 4 + y) * 2 + core) * 2 * HALF
    w_ref, enc_ref, refs = refs[0], refs[1], refs[2:]
    if not first:
        total_ref, refs = refs[0], refs[1:]
    if last:
        refs, (narrow, out_sems) = refs[:-2], refs[-2:]
    outs, (q_all, grads, bits) = refs[:-3], refs[-3:]
    n_enc = 1 + max(out for out, _ in enc_at)
    encs, outs = outs[:n_enc], outs[n_enc:]
    if first:
        wet_ref, outs = outs[0], outs[1:]
        encode(w_ref, enc_ref, wet_ref)
    else:
        wet_ref = enc_ref
    for i in range(n):
        bufs, q_refs = q_refs[: parts[i]], q_refs[parts[i] :]
        size = 512 // parts[i]
        for j, buf in enumerate(bufs):
            at = 512 * i + size * j
            q_all[at : at + size, :] = buf[:size, :]
        tail = bufs[-1][size : size + TAIL, :].astype(F32).astype(I32)
        for b in range(4):
            lanes = slice(512 * i + 128 * b, 512 * i + 128 * b + 128)
            for w, word in enumerate(target_bits(tail, b, base)):
                bits[w, :, lanes] = word
    group = lax.broadcasted_iota(I32, (32, 1, 1), 0)
    for i in range(2):
        rows = slice(i * HALF, (i + 1) * HALF)
        for j in range(n):
            lanes = slice(512 * j, 512 * j + 512)
            logits = lax.dot_general(
                w_ref[rows, :], q_all[lanes, :], (((1,), (1,)), ((), ())), preferred_element_type=F32
            )
            for w in range(2):
                hit = (bits[2 * i + w, :, lanes][None] >> group) & 1
                target = hit.reshape(256, 512).astype(F32)
                some = jax.nn.sigmoid(logits[w * 256 : w * 256 + 256]) - target
                grads[i * HALF + w * 256 : i * HALF + w * 256 + 256, lanes] = (some * scale).astype(BF16)
        if not last:
            part = jnp.dot(grads[rows, :], q_all[...], preferred_element_type=F32)
            for c in range(4):
                columns = slice(256 * c, 256 * c + 256)
                old = 0.0 if first else total_ref[c, rows, :]
                outs[0][c, rows, :] = old + part[:, columns]
    encoded = jnp.dot(wet_ref[...], grads[...], preferred_element_type=F32)
    encoded = encoded[:192] + encoded[192:]
    for i, (out, column) in enumerate(enc_at):
        encs[out][:, column : column + 512] = encoded[:, 512 * i : 512 * i + 512]
    if last:
        copies = []
        for o, c in enumerate(quarters(x, core)):
            columns = q_all[:, pl.ds(pl.multiple_of(c * 256, 256), 256)]
            whole = total_ref[c] + jnp.dot(grads[...], columns, preferred_element_type=F32)
            narrow[o] = whole.astype(BF16)
            copies.append(pltpu.make_async_copy(narrow.at[o], outs[o], out_sems.at[o]))
            copies[-1].start()
        for copy in copies:
            copy.wait()


def chunk(place, groups, enc_at, w, enc, total, last, scale):
    first = total is None
    vmem = pl.BlockSpec(memory_space=pltpu.VMEM)
    widths = [0] * (1 + max(out for out, _ in enc_at))
    for out, column in enc_at:
        widths[out] = max(widths[out], column + 512)
    args = [place, *sum(groups, []), w, enc] + ([] if first else [total])
    labels = 2 * HALF
    shapes = [jax.ShapeDtypeStruct((192, n), F32) for n in widths]
    if first:
        shapes.append(jax.ShapeDtypeStruct((384, labels), BF16))
    if last:
        shapes += [jax.ShapeDtypeStruct((labels, 256), d) for d in (BF16,) * 4]
    else:
        shapes.append(jax.ShapeDtypeStruct((4, labels, 256), F32))
    n = 512 * len(enc_at)
    out_specs, scratch = [vmem] * len(shapes), []
    if last:
        out_specs[-4:] = [pl.BlockSpec(memory_space=pltpu.HBM)] * 4
        scratch = [pltpu.VMEM((4, labels, 256), BF16), pltpu.SemaphoreType.DMA((4,))]
    return pl.pallas_call(
        functools.partial(chunk_kernel, [len(g) for g in groups], enc_at, first, last, scale),
        in_specs=[pl.BlockSpec(memory_space=pltpu.SMEM)] + [vmem] * (len(args) - 1),
        out_specs=out_specs,
        out_shape=shapes,
        scratch_shapes=[
            pltpu.VMEM((n, 1024), BF16),
            pltpu.VMEM((labels, n), BF16),
            pltpu.VMEM((4, 8, n), I32),
            *scratch,
        ],
        input_output_aliases={} if first or last else {len(args) - 1: len(shapes) - 1},
        compiler_params=pltpu.CompilerParams(vmem_limit_bytes=VMEM_LIMIT),
        cost_estimate=pl.CostEstimate(
            flops=2 * n * labels * (2 * 1024 + 384), bytes_accessed=2**20, transcendentals=0
        ),
        name="chunk",
    )(*args)


def pack_kernel(place, *refs):
    own, sib, out = refs[:3], refs[3:6], refs[6]
    z, y, core = place[0], place[1], place[3]
    first, second = jnp.where(core == 0, z, y), jnp.where(core == 0, y, z)
    at = [(i, j) for i in OFFSETS for j in OFFSETS]
    for a, b in zip(own, sib):
        value = (a[...] + b[...]).astype(BF16)
        for block in range(value.shape[1] // 128):
            i, j = at.pop(0)
            j, i = lax.rem(first + j, 4), lax.rem(second + i, 4)
            out[jnp.where(core == 0, j * 4 + i, i * 4 + j)] = value[:, block * 128 : block * 128 + 128]


def decode_kernel(parts_ref, dec_ref, after_ref, out_ref):
    total = parts_ref[0].astype(F32)
    for i in range(1, 16):
        total += parts_ref[i].astype(F32)
    rest, result = total, None
    for _ in range(3):
        digit = rest.astype(BF16)
        rest = rest - digit.astype(F32)
        part = lax.dot_general(digit, dec_ref[...], (((0,), (0,)), ((), ())), preferred_element_type=F32)
        result = part if result is None else result + part
    out_ref[...] = result.astype(BF16)


def join_kernel(*refs):
    total = refs[0][...].astype(F32)
    for ref in refs[1:4]:
        total += ref[...].astype(F32)
    refs[4][...] = total.astype(BF16)
    refs[5][...] = jnp.zeros_like(refs[5])


def kernel(body, out, *args, name, flops=10**6):
    place = lambda a: pltpu.SMEM if a.shape == (4,) else pltpu.VMEM
    one = not isinstance(out[0][0], tuple)
    shapes = [jax.ShapeDtypeStruct(*o) for o in ([out] if one else out)]
    result = pl.pallas_call(
        body,
        in_specs=[pl.BlockSpec(memory_space=place(a)) for a in args],
        out_specs=[pl.BlockSpec(memory_space=pltpu.VMEM)] * len(shapes),
        out_shape=shapes,
        compiler_params=pltpu.CompilerParams(vmem_limit_bytes=VMEM_LIMIT),
        cost_estimate=pl.CostEstimate(flops=flops, bytes_accessed=2**10, transcendentals=0),
        name=name,
    )(*args)
    return result[0] if one else result


def after(arrays, *others):
    anywhere = pl.BlockSpec(memory_space=pl.ANY)
    n = len(arrays)
    tied = pl.pallas_call(
        lambda *refs: None,
        in_specs=[anywhere] * (n + len(others)),
        out_specs=[anywhere] * n,
        out_shape=[jax.ShapeDtypeStruct(a.shape, a.dtype) for a in arrays],
        input_output_aliases={i: i for i in range(n)},
        compiler_params=pltpu.CompilerParams(vmem_limit_bytes=2**20),
        cost_estimate=pl.CostEstimate(flops=0, bytes_accessed=0, transcendentals=0),
        name="after",
    )(*arrays, *others)
    return list(tied)


def shards(queries, label_ids, label_counts, weights, encoder, decoder):
    z, y, xl, xh, core = (lax.axis_index(a) for a in AXES)
    scale = float(queries.shape[0] * 128) ** (-0.5)

    slot = lax.broadcasted_iota(I32, (8, 128), 0)
    ids = jnp.where(slot < label_counts[None, :], label_ids.T, 255 * 256).reshape(1, 1024)
    tail = jnp.concatenate([ids >> 8, ids & 255, jnp.zeros((TAIL - 2, 1024), I32)], axis=0)
    own = jnp.concatenate([queries, tail.astype(BF16)], axis=0)

    place = jnp.stack([z, y, 2 * xh + xl, core]).astype(I32)
    w = move(weights, to_user)
    back, ahead, far = (move(own, hop(0, step)) for step in (1, -1, 2))
    row = kernel(row_kernel, ((512 + TAIL, 1024), BF16), place, own, back, ahead, far, name="row")
    row_back, row_ahead = move(row, hop(1, 1)), move(row, hop(1, -1))
    sibling = lambda bufs: [move(b, to_sibling) for b in bufs]
    apart, joined = ((0, 0), (1, 0)), ((0, 0), (0, 512))
    enc_a, enc_sa, wet, total = chunk(
        place, [[row], sibling([row])], apart, w, encoder.T, None, False, scale
    )
    half_shapes = (((256, 1024), BF16), ((256 + TAIL, 1024), BF16))
    row_back, row_ahead = after([row_back, row_ahead], wet)
    low, high = kernel(halves_kernel, half_shapes, row_back, row_ahead, name="halves")
    far = [move(low, hop(1, 1)), move(high, hop(1, -1))]
    enc_b, total = chunk(place, [[row_back], [row_ahead]], joined, w, wet, total, False, scale)
    enc_sb, total = chunk(
        place, [sibling([row_back]), sibling([row_ahead])], joined, w, wet, total, False, scale
    )
    far = after(far, enc_sb)
    enc_c, enc_sc, out_0, out_1, out_2, out_3 = chunk(
        place, [far, sibling(far)], apart, w, wet, total, True, scale
    )

    pick = lambda same, other: lambda z, y, x, c: same(z, y, x, c) if c == x % 2 else other(z, y, x, c)
    got = [
        move(out_0, pick(lambda z, y, x, c: (z, y, x + 2, 1 - c), lambda z, y, x, c: (z, y, x + 1, c))),
        move(out_1, pick(to_sibling, lambda z, y, x, c: (z, y, x - 1, c))),
        move(out_2, pick(lambda z, y, x, c: (z, y, x + 2, c), lambda z, y, x, c: (z, y, x + 1, 1 - c))),
        move(out_3, pick(lambda z, y, x, c: (z, y, x, c), lambda z, y, x, c: (z, y, x - 1, 1 - c))),
    ]

    packed = kernel(
        pack_kernel, ((16, 192, 128), BF16), place, enc_a, enc_b, enc_c, *sibling([enc_sa, enc_sb, enc_sc]), name="pack"
    )
    parts = lax.all_to_all(packed, ("z", "y"), split_axis=0, concat_axis=0, tiled=True)
    shapes = (((2 * HALF, 256), BF16), ((8, 128), F32))
    weight_grad, done = kernel(join_kernel, shapes, *got, name="join", flops=10**11)
    query_grad = kernel(decode_kernel, ((128, 1024), BF16), parts, decoder, done, name="decode")
    return query_grad, weight_grad


def solution(mesh):
    fine = Mesh(mesh.devices.reshape(4, 4, 2, 2, 2), AXES)
    label, dp = AXES[:3], AXES[3:]
    return jax.shard_map(
        shards,
        mesh=fine,
        in_specs=(P(AXES, None), P(AXES, None), P(AXES), P(label, None), P(), P()),
        out_specs=(P(AXES, None), P(label, dp)),
        check_vma=False,
    )
```

```python
import functools
import itertools

import jax
import jax.numpy as jnp
from jax import lax
from jax.experimental import pallas as pl
from jax.experimental.pallas import tpu as pltpu
from jax.sharding import Mesh, PartitionSpec as P

AXES = ("z", "y", "xl", "xh", "core")
BF16, F32, I32 = jnp.bfloat16, jnp.float32, jnp.int32
TAIL = 16
HALF = 512
VMEM_LIMIT = 16 * 2**20
OFFSETS = (0, 3, 1, 2)


def pairs(target):
    flat = lambda z, y, x, c: (((z % 4 * 4 + y % 4) * 2 + x % 2) * 2 + x % 4 // 2) * 2 + c
    places = itertools.product(range(4), range(4), range(4), range(2))
    return [(flat(*at), flat(*target(*at))) for at in places if target(*at) is not None]


def move(array, target):
    return lax.ppermute(array, AXES, pairs(target))


def hop(phase, step):
    return lambda z, y, x, c: (z + step, y, x, c) if c == phase else (z, y + step, x, c)


def to_sibling(z, y, x, c):
    return z, y, x, 1 - c


def to_user(z, y, x, c):
    return (z, y, x ^ 1, c) if c == x % 2 else (z, y, x, 1 - c)


def rows_kernel(place, own_ref, back_ref, ahead_ref, far_ref, low_ref, high_ref):
    refs = (own_ref, back_ref, ahead_ref, far_ref)
    for i, ref in enumerate(refs):
        half_ref = high_ref if i // 2 else low_ref
        half_ref[i % 2 * 128 : i % 2 * 128 + 128, :] = ref[:128, :]
    row = lax.broadcasted_iota(I32, (TAIL, 1024), 0)
    tail = jnp.zeros((TAIL, 1024), F32)
    for i, ref in enumerate(refs):
        ids = ref[128:144, :].astype(F32)
        for digit in range(2):
            tail = jnp.where(row == 2 * i + digit, ids[digit : digit + 1, :], tail)
    high_ref[256:, :] = tail.astype(BF16)


def encode(w_ref, enc_ref, wet_ref):
    we = lax.dot_general(
        enc_ref[...], w_ref[...], (((1,), (1,)), ((), ())), preferred_element_type=F32
    )
    high = we.astype(BF16)
    wet_ref[:192, :] = high
    wet_ref[192:, :] = (we - high.astype(F32)).astype(BF16)


def target_bits(tail, block, base):
    digits = tail[2 * block : 2 * block + 2, :]
    local = (digits[0:1] * 256 + digits[1:2]) - base
    low, bit = local & 7, jnp.left_shift(1, (local >> 3) & 31)
    words = [jnp.where((local >> 8) == w, bit, 0) for w in range(4)]
    row = lax.broadcasted_iota(I32, (8, 128), 0)
    bits = [jnp.zeros((8, 128), I32)] * 4
    for slot in range(8):
        lanes = slice(slot * 128, (slot + 1) * 128)
        here = jnp.broadcast_to(low[:, lanes], (8, 128)) == row
        for w in range(4):
            word = jnp.broadcast_to(words[w][:, lanes], (8, 128))
            bits[w] = bits[w] | jnp.where(here, word, 0)
    return bits


def quarters(x, core):
    keeps = core == lax.rem(x, 2)
    half, next_half = x // 2, lax.rem(x + 1, 4) // 2
    away = jnp.where(keeps, 1 - half, next_half)
    column = jnp.where(keeps, 1 - core, core)
    return 2 * away + column, 2 * (1 - away) + column, 2 * away + 1 - column, 2 * (1 - away) + 1 - column


def chunk_kernel(enc_at, fresh, first, last, scale, *refs):
    n = len(enc_at)
    place, q_refs, refs = refs[0], refs[1 : 1 + 2 * n], refs[1 + 2 * n :]
    z, y, x, core = (place[i] for i in range(4))
    base = ((z * 4 + y) * 2 + core) * 2 * HALF
    w_ref, enc_ref, refs = refs[0], refs[1], refs[2:]
    if not first:
        total_ref, refs = refs[0], refs[1:]
    sums = sorted({out for out, _ in enc_at})
    if not fresh:
        refs = refs[len(sums) :]
    if last:
        refs, (narrow, out_sems) = refs[:-2], refs[-2:]
    outs, (q_all, grads, bits) = refs[:-3], refs[-3:]
    encs, outs = dict(zip(sums, outs)), outs[len(sums) :]
    if first:
        wet_ref, outs = outs[0], outs[1:]
        encode(w_ref, enc_ref, wet_ref)
    else:
        wet_ref = enc_ref
    for i in range(n):
        low, high = q_refs[2 * i : 2 * i + 2]
        q_all[512 * i : 512 * i + 256, :] = low[...]
        q_all[512 * i + 256 : 512 * i + 512, :] = high[:256, :]
        tail = high[256:, :].astype(F32).astype(I32)
        for b in range(4):
            lanes = slice(512 * i + 128 * b, 512 * i + 128 * b + 128)
            for w, word in enumerate(target_bits(tail, b, base)):
                bits[w, :, lanes] = word
    group = lax.broadcasted_iota(I32, (32, 1, 1), 0)
    for i in range(2):
        rows = slice(i * HALF, (i + 1) * HALF)
        for j in range(n):
            lanes = slice(512 * j, 512 * j + 512)
            logits = lax.dot_general(
                w_ref[rows, :], q_all[lanes, :], (((1,), (1,)), ((), ())), preferred_element_type=F32
            )
            for w in range(2):
                hit = (bits[2 * i + w, :, lanes][None] >> group) & 1
                target = hit.reshape(256, 512).astype(F32)
                some = jax.nn.sigmoid(logits[w * 256 : w * 256 + 256]) - target
                grads[i * HALF + w * 256 : i * HALF + w * 256 + 256, lanes] = (some * scale).astype(BF16)
        if not last:
            part = jnp.dot(grads[rows, :], q_all[...], preferred_element_type=F32)
            for c in range(4):
                columns = slice(256 * c, 256 * c + 256)
                old = 0.0 if first else total_ref[c, rows, :]
                outs[0][c, rows, :] = old + part[:, columns]
    if last:
        copies = []
        for o, c in enumerate(quarters(x, core)):
            columns = q_all[:, pl.ds(pl.multiple_of(c * 256, 256), 256)]
            whole = total_ref[c] + jnp.dot(grads[...], columns, preferred_element_type=F32)
            narrow[o] = whole.astype(BF16)
            copies.append(pltpu.make_async_copy(narrow.at[o], outs[o], out_sems.at[o]))
            copies[-1].start()
    encoded = jnp.dot(wet_ref[...], grads[...], preferred_element_type=F32)
    encoded = encoded[:192] + encoded[192:]
    for i, (out, column) in enumerate(enc_at):
        encs[out][:, column : column + 512] = encoded[:, 512 * i : 512 * i + 512]
    if last:
        for copy in copies:
            copy.wait()


def chunk(place, groups, enc_at, w, enc, total, sums, last, scale):
    first, fresh = total is None, sums is None
    vmem = pl.BlockSpec(memory_space=pltpu.VMEM)
    labels, n = 2 * HALF, 512 * len(enc_at)
    named = sorted({out for out, _ in enc_at})
    args = [place, *sum(groups, []), w, enc] + ([] if first else [total])
    shapes = [jax.ShapeDtypeStruct((192, 2048), F32) for _ in named]
    aliases = {} if fresh else {len(args) + i: i for i in range(len(named))}
    if first:
        shapes.append(jax.ShapeDtypeStruct((384, labels), BF16))
    if last:
        shapes += [jax.ShapeDtypeStruct((labels, 256), BF16)] * 4
    else:
        if not first:
            aliases[len(args) - 1] = len(shapes)
        shapes.append(jax.ShapeDtypeStruct((4, labels, 256), F32))
    if not fresh:
        args += [sums[i] for i in named]
    out_specs, scratch = [vmem] * len(shapes), []
    if last:
        out_specs[-4:] = [pl.BlockSpec(memory_space=pltpu.HBM)] * 4
        scratch = [pltpu.VMEM((4, labels, 256), BF16), pltpu.SemaphoreType.DMA((4,))]
    out = pl.pallas_call(
        functools.partial(chunk_kernel, enc_at, fresh, first, last, scale),
        in_specs=[pl.BlockSpec(memory_space=pltpu.SMEM)] + [vmem] * (len(args) - 1),
        out_specs=out_specs,
        out_shape=shapes,
        scratch_shapes=[
            pltpu.VMEM((n, 1024), BF16),
            pltpu.VMEM((labels, n), BF16),
            pltpu.VMEM((4, 8, n), I32),
            *scratch,
        ],
        input_output_aliases=aliases,
        compiler_params=pltpu.CompilerParams(vmem_limit_bytes=VMEM_LIMIT),
        cost_estimate=pl.CostEstimate(
            flops=2 * n * labels * (2 * 1024 + 384), bytes_accessed=2**20, transcendentals=0
        ),
        name="chunk",
    )(*args)
    new = dict(enumerate([None, None] if fresh else sums)) | dict(zip(named, out))
    return ([new[0], new[1]], *out[len(named) :])


def pack_kernel(place, *refs):
    own, sib, out = refs
    z, y, core = place[0], place[1], place[3]
    first, second = jnp.where(core == 0, z, y), jnp.where(core == 0, y, z)
    for part in range(4):
        for block in range(4):
            lanes = slice(512 * part + 128 * block, 512 * part + 128 * block + 128)
            j, i = lax.rem(first + OFFSETS[block], 4), lax.rem(second + OFFSETS[part], 4)
            out[jnp.where(core == 0, j * 4 + i, i * 4 + j)] = (own[:, lanes] + sib[:, lanes]).astype(BF16)


def decode_kernel(parts_ref, dec_ref, after_ref, out_ref):
    total = parts_ref[0].astype(F32)
    for i in range(1, 16):
        total += parts_ref[i].astype(F32)
    rest, result = total, None
    for _ in range(3):
        digit = rest.astype(BF16)
        rest = rest - digit.astype(F32)
        part = lax.dot_general(digit, dec_ref[...], (((0,), (0,)), ((), ())), preferred_element_type=F32)
        result = part if result is None else result + part
    out_ref[...] = result.astype(BF16)


def join_kernel(*refs):
    total = refs[0][...].astype(F32)
    for ref in refs[1:4]:
        total += ref[...].astype(F32)
    refs[4][...] = total.astype(BF16)
    refs[5][...] = jnp.zeros_like(refs[5])


def kernel(body, out, *args, name, flops=10**6):
    place = lambda a: pltpu.SMEM if a.shape == (4,) else pltpu.VMEM
    one = not isinstance(out[0][0], tuple)
    shapes = [jax.ShapeDtypeStruct(*o) for o in ([out] if one else out)]
    result = pl.pallas_call(
        body,
        in_specs=[pl.BlockSpec(memory_space=place(a)) for a in args],
        out_specs=[pl.BlockSpec(memory_space=pltpu.VMEM)] * len(shapes),
        out_shape=shapes,
        compiler_params=pltpu.CompilerParams(vmem_limit_bytes=VMEM_LIMIT),
        cost_estimate=pl.CostEstimate(flops=flops, bytes_accessed=2**10, transcendentals=0),
        name=name,
    )(*args)
    return result[0] if one else result


def after(arrays, *others):
    anywhere = pl.BlockSpec(memory_space=pl.ANY)
    n = len(arrays)
    tied = pl.pallas_call(
        lambda *refs: None,
        in_specs=[anywhere] * (n + len(others)),
        out_specs=[anywhere] * n,
        out_shape=[jax.ShapeDtypeStruct(a.shape, a.dtype) for a in arrays],
        input_output_aliases={i: i for i in range(n)},
        compiler_params=pltpu.CompilerParams(vmem_limit_bytes=2**20),
        cost_estimate=pl.CostEstimate(flops=0, bytes_accessed=0, transcendentals=0),
        name="after",
    )(*arrays, *others)
    return list(tied)


def shards(queries, label_ids, label_counts, weights, encoder, decoder):
    z, y, xl, xh, core = (lax.axis_index(a) for a in AXES)
    scale = float(queries.shape[0] * 128) ** (-0.5)

    slot = lax.broadcasted_iota(I32, (8, 128), 0)
    ids = jnp.where(slot < label_counts[None, :], label_ids.T, 255 * 256).reshape(1, 1024)
    tail = jnp.concatenate([ids >> 8, ids & 255, jnp.zeros((TAIL - 2, 1024), I32)], axis=0)
    block = jnp.concatenate([queries, tail.astype(BF16)], axis=0)

    place = jnp.stack([z, y, 2 * xh + xl, core]).astype(I32)
    w = move(weights, to_user)
    back, ahead, far = (move(block, hop(0, step)) for step in (1, -1, 2))
    half_shapes = (((256, 1024), BF16), ((256 + TAIL, 1024), BF16))
    low, high = kernel(rows_kernel, half_shapes, place, block, back, ahead, far, name="rows")
    low_back, high_ahead = move(low, hop(1, 1)), move(high, hop(1, -1))
    high_back, low_ahead = move(high, hop(1, 1)), move(low, hop(1, -1))
    sibling = lambda array: move(array, to_sibling)
    row, own, sib = [low, high], 0, 1
    sums, wet, total = chunk(
        place, [row, [sibling(low), sibling(high)]], ((own, 0), (sib, 0)), w, encoder.T, None, None, False, scale
    )
    low_back, high_ahead = after([low_back, high_ahead], wet)
    far = [move(low_back, hop(1, 1)), move(high_ahead, hop(1, -1))]
    early = [sibling(low_back), sibling(high_ahead)]
    high_back, low_ahead = after([high_back, low_ahead], *early)
    late = [sibling(high_back), sibling(low_ahead)]
    back, ahead = [low_back, high_back], [low_ahead, high_ahead]
    sums, total = chunk(place, [back, ahead], ((own, 512), (own, 1024)), w, wet, total, sums, False, scale)
    far = after(far, sums[own])
    back, ahead = [early[0], late[0]], [late[1], early[1]]
    sums, total = chunk(place, [back, ahead], ((sib, 512), (sib, 1024)), w, wet, total, sums, False, scale)
    far_sib = [sibling(f) for f in far]
    sums, *outs = chunk(place, [far, far_sib], ((own, 1536), (sib, 1536)), w, wet, total, sums, True, scale)

    pick = lambda same, other: lambda z, y, x, c: same(z, y, x, c) if c == x % 2 else other(z, y, x, c)
    got = [
        move(outs[0], pick(lambda z, y, x, c: (z, y, x + 2, 1 - c), lambda z, y, x, c: (z, y, x + 1, c))),
        move(outs[1], pick(to_sibling, lambda z, y, x, c: (z, y, x - 1, c))),
        move(outs[2], pick(lambda z, y, x, c: (z, y, x + 2, c), lambda z, y, x, c: (z, y, x + 1, 1 - c))),
        move(outs[3], pick(lambda z, y, x, c: (z, y, x, c), lambda z, y, x, c: (z, y, x - 1, 1 - c))),
    ]

    packed = kernel(pack_kernel, ((16, 192, 128), BF16), place, sums[own], sibling(sums[sib]), name="pack")
    parts = lax.all_to_all(packed, ("z", "y"), split_axis=0, concat_axis=0, tiled=True)
    shapes = (((2 * HALF, 256), BF16), ((8, 128), F32))
    weight_grad, done = kernel(join_kernel, shapes, *got, name="join", flops=10**11)
    query_grad = kernel(decode_kernel, ((128, 1024), BF16), parts, decoder, done, name="decode")
    return query_grad, weight_grad


def solution(mesh):
    fine = Mesh(mesh.devices.reshape(4, 4, 2, 2, 2), AXES)
    label, dp = AXES[:3], AXES[3:]
    return jax.shard_map(
        shards,
        mesh=fine,
        in_specs=(P(AXES, None), P(AXES, None), P(AXES), P(label, None), P(), P()),
        out_specs=(P(AXES, None), P(label, dp)),
        check_vma=False,
    )
```

```python
import functools
import itertools

import jax
import jax.numpy as jnp
from jax import lax
from jax.experimental import pallas as pl
from jax.experimental.pallas import tpu as pltpu
from jax.sharding import Mesh, PartitionSpec as P

AXES = ("z", "y", "xl", "xh", "core")
BF16, F32, I32 = jnp.bfloat16, jnp.float32, jnp.int32
TAIL = 16
HALF = 512
VMEM_LIMIT = 16 * 2**20
OFFSETS = (0, 3, 1, 2)


def pairs(target):
    flat = lambda z, y, x, c: (((z % 4 * 4 + y % 4) * 2 + x % 2) * 2 + x % 4 // 2) * 2 + c
    places = itertools.product(range(4), range(4), range(4), range(2))
    return [(flat(*at), flat(*target(*at))) for at in places if target(*at) is not None]


def move(array, target):
    return lax.ppermute(array, AXES, pairs(target))


def hop(phase, step):
    return lambda z, y, x, c: (z + step, y, x, c) if c == phase else (z, y + step, x, c)


def to_sibling(z, y, x, c):
    return z, y, x, 1 - c


def to_user(z, y, x, c):
    return (z, y, x ^ 1, c) if c == x % 2 else (z, y, x, 1 - c)


def rows_kernel(place, own_ref, back_ref, ahead_ref, far_ref, low_ref, high_ref):
    refs = (own_ref, back_ref, ahead_ref, far_ref)
    for i, ref in enumerate(refs):
        half_ref = high_ref if i // 2 else low_ref
        half_ref[i % 2 * 128 : i % 2 * 128 + 128, :] = ref[:128, :]
    row = lax.broadcasted_iota(I32, (TAIL, 1024), 0)
    tail = jnp.zeros((TAIL, 1024), F32)
    for i, ref in enumerate(refs):
        ids = ref[128:144, :].astype(F32)
        for digit in range(2):
            tail = jnp.where(row == 2 * i + digit, ids[digit : digit + 1, :], tail)
    high_ref[256:, :] = tail.astype(BF16)


def encode(w_ref, enc_ref, wet_ref):
    we = lax.dot_general(
        enc_ref[...], w_ref[...], (((1,), (1,)), ((), ())), preferred_element_type=F32
    )
    high = we.astype(BF16)
    wet_ref[:192, :] = high
    wet_ref[192:, :] = (we - high.astype(F32)).astype(BF16)


def target_bits(tail, block, base):
    digits = tail[2 * block : 2 * block + 2, :]
    local = (digits[0:1] * 256 + digits[1:2]) - base
    low, bit = local & 7, jnp.left_shift(1, (local >> 3) & 31)
    words = [jnp.where((local >> 8) == w, bit, 0) for w in range(4)]
    row = lax.broadcasted_iota(I32, (8, 128), 0)
    bits = [jnp.zeros((8, 128), I32)] * 4
    for slot in range(8):
        lanes = slice(slot * 128, (slot + 1) * 128)
        here = jnp.broadcast_to(low[:, lanes], (8, 128)) == row
        for w in range(4):
            word = jnp.broadcast_to(words[w][:, lanes], (8, 128))
            bits[w] = bits[w] | jnp.where(here, word, 0)
    return bits


def quarters(x, core):
    keeps = core == lax.rem(x, 2)
    half, next_half = x // 2, lax.rem(x + 1, 4) // 2
    away = jnp.where(keeps, 1 - half, next_half)
    column = jnp.where(keeps, 1 - core, core)
    return 2 * away + column, 2 * (1 - away) + column, 2 * away + 1 - column, 2 * (1 - away) + 1 - column


def chunk_kernel(enc_at, stage, scale, *refs):
    n = len(enc_at)
    place, q_refs, refs = refs[0], refs[1 : 1 + 2 * n], refs[1 + 2 * n :]
    z, y, x, core = (place[i] for i in range(4))
    base = ((z * 4 + y) * 2 + core) * 2 * HALF
    w_ref, refs = refs[0], refs[1:]
    q_all, bits, refs = refs[-2], refs[-1], refs[:-2]
    if stage == 0:
        outs, grads = refs[:1], refs[1]
    else:
        grads, refs = refs[-1], refs[:-1]
        total_ref, enc_ref, refs = refs[0], refs[1], refs[2:]
        if stage == 3:
            refs, (narrow, out_sems) = refs[:-2], refs[-2:]
        if stage == 1:
            early, encs, wet_ref, outs = refs[0], refs[1:3], refs[3], refs[4:]
            encode(w_ref, enc_ref, wet_ref)
        else:
            wet_ref = enc_ref
            named = sorted({out for out, _ in enc_at})
            refs = refs[len(named) :]
            encs, outs = dict(zip(named, refs)), refs[len(named) :]
    for i in range(n):
        low, high = q_refs[2 * i : 2 * i + 2]
        q_all[512 * i : 512 * i + 256, :] = low[...]
        q_all[512 * i + 256 : 512 * i + 512, :] = high[:256, :]
        tail = high[256:, :].astype(F32).astype(I32)
        for b in range(4):
            lanes = slice(512 * i + 128 * b, 512 * i + 128 * b + 128)
            for w, word in enumerate(target_bits(tail, b, base)):
                bits[w, :, lanes] = word
    group = lax.broadcasted_iota(I32, (32, 1, 1), 0)
    for i in range(2):
        rows = slice(i * HALF, (i + 1) * HALF)
        for j in range(n):
            lanes = slice(512 * j, 512 * j + 512)
            logits = lax.dot_general(
                w_ref[rows, :], q_all[lanes, :], (((1,), (1,)), ((), ())), preferred_element_type=F32
            )
            for w in range(2):
                hit = (bits[2 * i + w, :, lanes][None] >> group) & 1
                target = hit.reshape(256, 512).astype(F32)
                some = jax.nn.sigmoid(logits[w * 256 : w * 256 + 256]) - target
                grads[i * HALF + w * 256 : i * HALF + w * 256 + 256, lanes] = (some * scale).astype(BF16)
        if stage != 3:
            part = jnp.dot(grads[rows, :], q_all[...], preferred_element_type=F32)
            for c in range(4):
                columns = slice(256 * c, 256 * c + 256)
                old = total_ref[c, rows, :] if stage else 0.0
                outs[0][c, rows, :] = old + part[:, columns]
    if stage == 0:
        return
    if stage == 3:
        copies = []
        for o, c in enumerate(quarters(x, core)):
            columns = q_all[:, pl.ds(pl.multiple_of(c * 256, 256), 256)]
            whole = total_ref[c] + jnp.dot(grads[...], columns, preferred_element_type=F32)
            narrow[o] = whole.astype(BF16)
            copies.append(pltpu.make_async_copy(narrow.at[o], outs[o], out_sems.at[o]))
            copies[-1].start()
    both = [(grads, enc_at)] + ([(early, ((0, 0), (1, 0)))] if stage == 1 else [])
    for values, to in both:
        encoded = jnp.dot(wet_ref[...], values[...], preferred_element_type=F32)
        encoded = encoded[:192] + encoded[192:]
        for i, (out, column) in enumerate(to):
            encs[out][:, column : column + 512] = encoded[:, 512 * i : 512 * i + 512]
    if stage == 3:
        for copy in copies:
            copy.wait()


def chunk(stage, place, groups, enc_at, w, scale, total=None, enc=None, early=None, sums=()):
    vmem = pl.BlockSpec(memory_space=pltpu.VMEM)
    labels, n = 2 * HALF, 512 * len(enc_at)
    named = sorted({out for out, _ in enc_at}) if stage > 1 else [0, 1]
    args = [place, *sum(groups, []), w] + ([total, enc] if stage else [])
    at_total = len(args) - 2
    shapes, aliases = [], {}
    if stage:
        shapes = [jax.ShapeDtypeStruct((192, 2048), F32) for _ in named]
    if stage == 1:
        args.append(early)
        shapes.append(jax.ShapeDtypeStruct((384, labels), BF16))
    if stage > 1:
        aliases = {len(args) + i: i for i in range(len(named))}
        args += [sums[i] for i in named]
    if stage == 3:
        shapes += [jax.ShapeDtypeStruct((labels, 256), BF16)] * 4
    else:
        if stage:
            aliases[at_total] = len(shapes)
        shapes.append(jax.ShapeDtypeStruct((4, labels, 256), F32))
    grads = [pltpu.VMEM((labels, n), BF16)]
    if stage == 0:
        shapes.append(jax.ShapeDtypeStruct((labels, n), BF16))
        grads = []
    out_specs, scratch = [vmem] * len(shapes), []
    if stage == 3:
        out_specs[-4:] = [pl.BlockSpec(memory_space=pltpu.HBM)] * 4
        scratch = [pltpu.VMEM((4, labels, 256), BF16), pltpu.SemaphoreType.DMA((4,))]
    out = pl.pallas_call(
        functools.partial(chunk_kernel, enc_at, stage, scale),
        in_specs=[pl.BlockSpec(memory_space=pltpu.SMEM)] + [vmem] * (len(args) - 1),
        out_specs=out_specs,
        out_shape=shapes,
        scratch_shapes=[*scratch, *grads, pltpu.VMEM((n, 1024), BF16), pltpu.VMEM((4, 8, n), I32)],
        input_output_aliases=aliases,
        compiler_params=pltpu.CompilerParams(vmem_limit_bytes=VMEM_LIMIT),
        cost_estimate=pl.CostEstimate(
            flops=2 * n * labels * (2 * 1024 + 384), bytes_accessed=2**20, transcendentals=0
        ),
        name="chunk",
    )(*args)
    if stage == 0:
        return out
    new = dict(enumerate(sums)) | dict(zip(named, out))
    return ([new[0], new[1]], *out[len(named) :])


def pack_kernel(place, *refs):
    own, sib, out = refs
    z, y, core = place[0], place[1], place[3]
    first, second = jnp.where(core == 0, z, y), jnp.where(core == 0, y, z)
    for part in range(4):
        for block in range(4):
            lanes = slice(512 * part + 128 * block, 512 * part + 128 * block + 128)
            j, i = lax.rem(first + OFFSETS[block], 4), lax.rem(second + OFFSETS[part], 4)
            out[jnp.where(core == 0, j * 4 + i, i * 4 + j)] = (own[:, lanes] + sib[:, lanes]).astype(BF16)


def decode_kernel(parts_ref, dec_ref, after_ref, out_ref):
    total = parts_ref[0].astype(F32)
    for i in range(1, 16):
        total += parts_ref[i].astype(F32)
    rest, result = total, None
    for _ in range(3):
        digit = rest.astype(BF16)
        rest = rest - digit.astype(F32)
        part = lax.dot_general(digit, dec_ref[...], (((0,), (0,)), ((), ())), preferred_element_type=F32)
        result = part if result is None else result + part
    out_ref[...] = result.astype(BF16)


def join_kernel(*refs):
    total = refs[0][...].astype(F32)
    for ref in refs[1:4]:
        total += ref[...].astype(F32)
    refs[4][...] = total.astype(BF16)
    refs[5][...] = jnp.zeros_like(refs[5])


def kernel(body, out, *args, name, flops=10**6):
    place = lambda a: pltpu.SMEM if a.shape == (4,) else pltpu.VMEM
    one = not isinstance(out[0][0], tuple)
    shapes = [jax.ShapeDtypeStruct(*o) for o in ([out] if one else out)]
    result = pl.pallas_call(
        body,
        in_specs=[pl.BlockSpec(memory_space=place(a)) for a in args],
        out_specs=[pl.BlockSpec(memory_space=pltpu.VMEM)] * len(shapes),
        out_shape=shapes,
        compiler_params=pltpu.CompilerParams(vmem_limit_bytes=VMEM_LIMIT),
        cost_estimate=pl.CostEstimate(flops=flops, bytes_accessed=2**10, transcendentals=0),
        name=name,
    )(*args)
    return result[0] if one else result


def after(arrays, *others):
    anywhere = pl.BlockSpec(memory_space=pl.ANY)
    n = len(arrays)
    tied = pl.pallas_call(
        lambda *refs: None,
        in_specs=[anywhere] * (n + len(others)),
        out_specs=[anywhere] * n,
        out_shape=[jax.ShapeDtypeStruct(a.shape, a.dtype) for a in arrays],
        input_output_aliases={i: i for i in range(n)},
        compiler_params=pltpu.CompilerParams(vmem_limit_bytes=2**20),
        cost_estimate=pl.CostEstimate(flops=0, bytes_accessed=0, transcendentals=0),
        name="after",
    )(*arrays, *others)
    return list(tied)


def shards(queries, label_ids, label_counts, weights, encoder, decoder):
    z, y, xl, xh, core = (lax.axis_index(a) for a in AXES)
    scale = float(queries.shape[0] * 128) ** (-0.5)

    slot = lax.broadcasted_iota(I32, (8, 128), 0)
    ids = jnp.where(slot < label_counts[None, :], label_ids.T, 255 * 256).reshape(1, 1024)
    tail = jnp.concatenate([ids >> 8, ids & 255, jnp.zeros((TAIL - 2, 1024), I32)], axis=0)
    block = jnp.concatenate([queries, tail.astype(BF16)], axis=0)

    place = jnp.stack([z, y, 2 * xh + xl, core]).astype(I32)
    w = move(weights, to_user)
    back, ahead, far = (move(block, hop(0, step)) for step in (1, -1, 2))
    half_shapes = (((256, 1024), BF16), ((256 + TAIL, 1024), BF16))
    low, high = kernel(rows_kernel, half_shapes, place, block, back, ahead, far, name="rows")
    low_back, high_ahead = move(low, hop(1, 1)), move(high, hop(1, -1))
    high_back, low_ahead = move(high, hop(1, 1)), move(low, hop(1, -1))
    sibling = lambda array: move(array, to_sibling)
    row, own, sib = [low, high], 0, 1
    rows = [row, [sibling(low), sibling(high)]]
    total, early_grads = chunk(0, place, rows, ((own, 0), (sib, 0)), w, scale)
    low_back, high_ahead = after([low_back, high_ahead], early_grads)
    far = [move(low_back, hop(1, 1)), move(high_ahead, hop(1, -1))]
    early = [sibling(low_back), sibling(high_ahead)]
    high_back, low_ahead = after([high_back, low_ahead], *early)
    late = [sibling(high_back), sibling(low_ahead)]
    back, ahead = [low_back, high_back], [low_ahead, high_ahead]
    sums, wet, total = chunk(
        1, place, [back, ahead], ((own, 512), (own, 1024)), w, scale, total, encoder.T, early_grads
    )
    far = after(far, sums[own])
    back, ahead = [early[0], late[0]], [late[1], early[1]]
    sums, total = chunk(2, place, [back, ahead], ((sib, 512), (sib, 1024)), w, scale, total, wet, None, sums)
    far_sib = [sibling(f) for f in far]
    sums, *outs = chunk(3, place, [far, far_sib], ((own, 1536), (sib, 1536)), w, scale, total, wet, None, sums)

    pick = lambda same, other: lambda z, y, x, c: same(z, y, x, c) if c == x % 2 else other(z, y, x, c)
    got = [
        move(outs[0], pick(lambda z, y, x, c: (z, y, x + 2, 1 - c), lambda z, y, x, c: (z, y, x + 1, c))),
        move(outs[1], pick(to_sibling, lambda z, y, x, c: (z, y, x - 1, c))),
        move(outs[2], pick(lambda z, y, x, c: (z, y, x + 2, c), lambda z, y, x, c: (z, y, x + 1, 1 - c))),
        move(outs[3], pick(lambda z, y, x, c: (z, y, x, c), lambda z, y, x, c: (z, y, x - 1, 1 - c))),
    ]

    packed = kernel(pack_kernel, ((16, 192, 128), BF16), place, sums[own], sibling(sums[sib]), name="pack")
    parts = lax.all_to_all(packed, ("z", "y"), split_axis=0, concat_axis=0, tiled=True)
    shapes = (((2 * HALF, 256), BF16), ((8, 128), F32))
    weight_grad, done = kernel(join_kernel, shapes, *got, name="join", flops=10**11)
    query_grad = kernel(decode_kernel, ((128, 1024), BF16), parts, decoder, done, name="decode")
    return query_grad, weight_grad


def solution(mesh):
    fine = Mesh(mesh.devices.reshape(4, 4, 2, 2, 2), AXES)
    label, dp = AXES[:3], AXES[3:]
    return jax.shard_map(
        shards,
        mesh=fine,
        in_specs=(P(AXES, None), P(AXES, None), P(AXES), P(label, None), P(), P()),
        out_specs=(P(AXES, None), P(label, dp)),
        check_vma=False,
    )
```

```python
import functools
import itertools

import jax
import jax.numpy as jnp
from jax import lax
from jax.experimental import pallas as pl
from jax.experimental.pallas import tpu as pltpu
from jax.sharding import Mesh, PartitionSpec as P

AXES = ("z", "y", "xl", "xh", "core")
BF16, F32, I32 = jnp.bfloat16, jnp.float32, jnp.int32
TAIL = 16
HALF = 512
VMEM_LIMIT = 12 * 2**20
OFFSETS = (0, 3, 1, 2)


def pairs(target):
    flat = lambda z, y, x, c: (((z % 4 * 4 + y % 4) * 2 + x % 2) * 2 + x % 4 // 2) * 2 + c
    places = itertools.product(range(4), range(4), range(4), range(2))
    return [(flat(*at), flat(*target(*at))) for at in places if target(*at) is not None]


def move(array, target):
    return lax.ppermute(array, AXES, pairs(target))


def hop(phase, step):
    return lambda z, y, x, c: (z + step, y, x, c) if c == phase else (z, y + step, x, c)


def to_sibling(z, y, x, c):
    return z, y, x, 1 - c


def to_user(z, y, x, c):
    return (z, y, x ^ 1, c) if c == x % 2 else (z, y, x, 1 - c)


def rows_kernel(place, own_ref, back_ref, ahead_ref, far_ref, low_ref, high_ref):
    refs = (own_ref, back_ref, ahead_ref, far_ref)
    for i, ref in enumerate(refs):
        half_ref = high_ref if i // 2 else low_ref
        half_ref[i % 2 * 128 : i % 2 * 128 + 128, :] = ref[:128, :]
    row = lax.broadcasted_iota(I32, (TAIL, 1024), 0)
    tail = jnp.zeros((TAIL, 1024), F32)
    for i, ref in enumerate(refs):
        ids = ref[128:144, :].astype(F32)
        for digit in range(2):
            tail = jnp.where(row == 2 * i + digit, ids[digit : digit + 1, :], tail)
    high_ref[256:, :] = tail.astype(BF16)


def encode(w_ref, enc_ref, wet_ref):
    we = lax.dot_general(
        enc_ref[...], w_ref[...], (((1,), (1,)), ((), ())), preferred_element_type=F32
    )
    high = we.astype(BF16)
    wet_ref[:192, :] = high
    wet_ref[192:, :] = (we - high.astype(F32)).astype(BF16)


def target_bits(tail, block, base):
    digits = tail[2 * block : 2 * block + 2, :]
    local = (digits[0:1] * 256 + digits[1:2]) - base
    low, bit = local & 7, jnp.left_shift(1, (local >> 3) & 31)
    words = [jnp.where((local >> 8) == w, bit, 0) for w in range(4)]
    row = lax.broadcasted_iota(I32, (8, 128), 0)
    bits = [jnp.zeros((8, 128), I32)] * 4
    for slot in range(8):
        lanes = slice(slot * 128, (slot + 1) * 128)
        here = jnp.broadcast_to(low[:, lanes], (8, 128)) == row
        for w in range(4):
            word = jnp.broadcast_to(words[w][:, lanes], (8, 128))
            bits[w] = bits[w] | jnp.where(here, word, 0)
    return bits


def quarters(x, core):
    keeps = core == lax.rem(x, 2)
    half, next_half = x // 2, lax.rem(x + 1, 4) // 2
    away = jnp.where(keeps, 1 - half, next_half)
    column = jnp.where(keeps, 1 - core, core)
    return 2 * away + column, 2 * (1 - away) + column, 2 * away + 1 - column, 2 * (1 - away) + 1 - column


def chunk_kernel(enc_at, stage, scale, *refs):
    n = len(enc_at)
    place, q_refs, refs = refs[0], refs[1 : 1 + 2 * n], refs[1 + 2 * n :]
    z, y, x, core = (place[i] for i in range(4))
    base = ((z * 4 + y) * 2 + core) * 2 * HALF
    w_ref, refs = refs[0], refs[1:]
    q_all, bits, refs = refs[-2], refs[-1], refs[:-2]
    if stage == 0:
        outs, grads = refs[:1], refs[1]
    else:
        grads, refs = refs[-1], refs[:-1]
        total_ref, wet_ref, refs = refs[0], refs[1], refs[2:]
        if stage == 3:
            refs, (narrow, out_sems) = refs[:-2], refs[-2:]
        named = sorted({out for out, _ in enc_at})
        refs = refs[len(named) :]
        encs, outs = dict(zip(named, refs)), refs[len(named) :]
    for i in range(n):
        low, high = q_refs[2 * i : 2 * i + 2]
        q_all[512 * i : 512 * i + 256, :] = low[...]
        q_all[512 * i + 256 : 512 * i + 512, :] = high[:256, :]
        tail = high[256:, :].astype(F32).astype(I32)
        for b in range(4):
            lanes = slice(512 * i + 128 * b, 512 * i + 128 * b + 128)
            for w, word in enumerate(target_bits(tail, b, base)):
                bits[w, :, lanes] = word
    group = lax.broadcasted_iota(I32, (32, 1, 1), 0)
    for i in range(2):
        rows = slice(i * HALF, (i + 1) * HALF)
        for j in range(n):
            lanes = slice(512 * j, 512 * j + 512)
            logits = lax.dot_general(
                w_ref[rows, :], q_all[lanes, :], (((1,), (1,)), ((), ())), preferred_element_type=F32
            )
            for w in range(2):
                hit = (bits[2 * i + w, :, lanes][None] >> group) & 1
                target = hit.reshape(256, 512).astype(F32)
                some = jax.nn.sigmoid(logits[w * 256 : w * 256 + 256]) - target
                grads[i * HALF + w * 256 : i * HALF + w * 256 + 256, lanes] = (some * scale).astype(BF16)
        if stage != 3:
            part = jnp.dot(grads[rows, :], q_all[...], preferred_element_type=F32)
            for c in range(4):
                columns = slice(256 * c, 256 * c + 256)
                old = total_ref[c, rows, :] if stage else 0.0
                outs[0][c, rows, :] = old + part[:, columns]
    if stage == 0:
        return
    if stage == 3:
        copies = []
        for o, c in enumerate(quarters(x, core)):
            columns = q_all[:, pl.ds(pl.multiple_of(c * 256, 256), 256)]
            whole = total_ref[c] + jnp.dot(grads[...], columns, preferred_element_type=F32)
            narrow[o] = whole.astype(BF16)
            copies.append(pltpu.make_async_copy(narrow.at[o], outs[o], out_sems.at[o]))
            copies[-1].start()
    encoded = jnp.dot(wet_ref[...], grads[...], preferred_element_type=F32)
    encoded = encoded[:192] + encoded[192:]
    for i, (out, column) in enumerate(enc_at):
        encs[out][:, column : column + 512] = encoded[:, 512 * i : 512 * i + 512]
    if stage == 3:
        for copy in copies:
            copy.wait()


def chunk(stage, place, groups, enc_at, w, scale, total=None, wet=None, sums=()):
    vmem = pl.BlockSpec(memory_space=pltpu.VMEM)
    labels, n = 2 * HALF, 512 * len(enc_at)
    named = sorted({out for out, _ in enc_at})
    args = [place, *sum(groups, []), w] + ([total, wet] if stage else [])
    at_total = len(args) - 2
    shapes, aliases = [], {}
    if stage:
        shapes = [jax.ShapeDtypeStruct((192, 2048), F32) for _ in named]
        aliases = {len(args) + i: i for i in range(len(named))}
        args += [sums[i] for i in named]
    if stage == 3:
        shapes += [pltpu.HBM((labels, 256), BF16)] * 4
    else:
        if stage:
            aliases[at_total] = len(shapes)
        shapes.append(jax.ShapeDtypeStruct((4, labels, 256), F32))
    grads = [pltpu.VMEM((labels, n), BF16)]
    if stage == 0:
        shapes.append(jax.ShapeDtypeStruct((labels, n), BF16))
        grads = []
    out_specs, scratch = [vmem] * len(shapes), []
    if stage == 3:
        out_specs[-4:] = [pl.BlockSpec(memory_space=pltpu.HBM)] * 4
        scratch = [pltpu.VMEM((4, labels, 256), BF16), pltpu.SemaphoreType.DMA((4,))]
    out = pl.pallas_call(
        functools.partial(chunk_kernel, enc_at, stage, scale),
        in_specs=[pl.BlockSpec(memory_space=pltpu.SMEM)] + [vmem] * (len(args) - 1),
        out_specs=out_specs,
        out_shape=shapes,
        scratch_shapes=[*scratch, *grads, pltpu.VMEM((n, 1024), BF16), pltpu.VMEM((4, 8, n), I32)],
        input_output_aliases=aliases,
        compiler_params=pltpu.CompilerParams(vmem_limit_bytes=VMEM_LIMIT),
        cost_estimate=pl.CostEstimate(
            flops=2 * n * labels * (2 * 1024 + 384), bytes_accessed=2**20, transcendentals=0
        ),
        name="chunk",
    )(*args)
    if stage == 0:
        return out
    new = dict(enumerate(sums)) | dict(zip(named, out))
    return ([new[0], new[1]], *out[len(named) :])


def early_kernel(w_ref, enc_ref, grads_ref, own_ref, sib_ref, wet_ref):
    encode(w_ref, enc_ref, wet_ref)
    encoded = jnp.dot(wet_ref[...], grads_ref[...], preferred_element_type=F32)
    encoded = encoded[:192] + encoded[192:]
    own_ref[:, :512] = encoded[:, :512]
    sib_ref[:, :512] = encoded[:, 512:]


def pack_kernel(place, *refs):
    own, sib, out = refs
    z, y, core = place[0], place[1], place[3]
    first, second = jnp.where(core == 0, z, y), jnp.where(core == 0, y, z)
    for part in range(4):
        for block in range(4):
            lanes = slice(512 * part + 128 * block, 512 * part + 128 * block + 128)
            j, i = lax.rem(first + OFFSETS[block], 4), lax.rem(second + OFFSETS[part], 4)
            out[jnp.where(core == 0, j * 4 + i, i * 4 + j)] = (own[:, lanes] + sib[:, lanes]).astype(BF16)


def decode_kernel(parts_ref, dec_ref, after_ref, out_ref):
    total = parts_ref[0].astype(F32)
    for i in range(1, 16):
        total += parts_ref[i].astype(F32)
    rest, result = total, None
    for _ in range(3):
        digit = rest.astype(BF16)
        rest = rest - digit.astype(F32)
        part = lax.dot_general(digit, dec_ref[...], (((0,), (0,)), ((), ())), preferred_element_type=F32)
        result = part if result is None else result + part
    out_ref[...] = result.astype(BF16)


def join_kernel(*refs):
    total = refs[0][...].astype(F32)
    for ref in refs[1:4]:
        total += ref[...].astype(F32)
    refs[4][...] = total.astype(BF16)
    refs[5][...] = jnp.zeros_like(refs[5])


def kernel(body, out, *args, name, flops=10**6):
    place = lambda a: pltpu.SMEM if a.shape == (4,) else pltpu.VMEM
    one = not isinstance(out[0][0], tuple)
    shapes = [jax.ShapeDtypeStruct(*o) for o in ([out] if one else out)]
    result = pl.pallas_call(
        body,
        in_specs=[pl.BlockSpec(memory_space=place(a)) for a in args],
        out_specs=[pl.BlockSpec(memory_space=pltpu.VMEM)] * len(shapes),
        out_shape=shapes,
        compiler_params=pltpu.CompilerParams(vmem_limit_bytes=VMEM_LIMIT),
        cost_estimate=pl.CostEstimate(flops=flops, bytes_accessed=2**10, transcendentals=0),
        name=name,
    )(*args)
    return result[0] if one else result


def after(arrays, *others):
    anywhere = pl.BlockSpec(memory_space=pl.ANY)
    n = len(arrays)
    tied = pl.pallas_call(
        lambda *refs: None,
        in_specs=[anywhere] * (n + len(others)),
        out_specs=[anywhere] * n,
        out_shape=[jax.ShapeDtypeStruct(a.shape, a.dtype) for a in arrays],
        input_output_aliases={i: i for i in range(n)},
        compiler_params=pltpu.CompilerParams(vmem_limit_bytes=2**20),
        cost_estimate=pl.CostEstimate(flops=0, bytes_accessed=0, transcendentals=0),
        name="after",
    )(*arrays, *others)
    return list(tied)


def shards(queries, label_ids, label_counts, weights, encoder, decoder):
    z, y, xl, xh, core = (lax.axis_index(a) for a in AXES)
    scale = float(queries.shape[0] * 128) ** (-0.5)

    slot = lax.broadcasted_iota(I32, (8, 128), 0)
    ids = jnp.where(slot < label_counts[None, :], label_ids.T, 255 * 256).reshape(1, 1024)
    tail = jnp.concatenate([ids >> 8, ids & 255, jnp.zeros((TAIL - 2, 1024), I32)], axis=0)
    block = jnp.concatenate([queries, tail.astype(BF16)], axis=0)

    place = jnp.stack([z, y, 2 * xh + xl, core]).astype(I32)
    w = move(weights, to_user)
    far, ahead, back = (move(block, hop(0, step)) for step in (2, -1, 1))
    half_shapes = (((256, 1024), BF16), ((256 + TAIL, 1024), BF16))
    low, high = kernel(rows_kernel, half_shapes, place, block, back, ahead, far, name="rows")
    low_back, high_ahead = move(low, hop(1, 1)), move(high, hop(1, -1))
    high_back, low_ahead = move(high, hop(1, 1)), move(low, hop(1, -1))
    sibling = lambda array: move(array, to_sibling)
    row, own, sib = [low, high], 0, 1
    rows = [row, [sibling(low), sibling(high)]]
    total, early_grads = chunk(0, place, rows, ((own, 0), (sib, 0)), w, scale)
    sums_wet = kernel(
        early_kernel,
        (((192, 2048), F32), ((192, 2048), F32), ((384, 2 * HALF), BF16)),
        w, encoder.T, early_grads, name="early", flops=2 * 1024 * 1024 * 512,
    )
    low_back, high_ahead = after([low_back, high_ahead], early_grads)
    far = [move(low_back, hop(1, 1)), move(high_ahead, hop(1, -1))]
    early = [sibling(low_back), sibling(high_ahead)]
    high_back, low_ahead = after([high_back, low_ahead], *early, sums_wet[2])
    late = [sibling(high_back), sibling(low_ahead)]
    back, ahead = [low_back, high_back], [low_ahead, high_ahead]
    sums, wet = sums_wet[:2], sums_wet[2]
    sums, total = chunk(1, place, [back, ahead], ((own, 512), (own, 1024)), w, scale, total, wet, sums)
    far = after(far, sums[own])
    back, ahead = [early[0], late[0]], [late[1], early[1]]
    sums, total = chunk(2, place, [back, ahead], ((sib, 512), (sib, 1024)), w, scale, total, wet, sums)
    far_sib = [sibling(f) for f in far]
    sums, *outs = chunk(3, place, [far, far_sib], ((own, 1536), (sib, 1536)), w, scale, total, wet, sums)

    pick = lambda same, other: lambda z, y, x, c: same(z, y, x, c) if c == x % 2 else other(z, y, x, c)
    got = [
        move(outs[0], pick(lambda z, y, x, c: (z, y, x + 2, 1 - c), lambda z, y, x, c: (z, y, x + 1, c))),
        move(outs[2], pick(lambda z, y, x, c: (z, y, x + 2, c), lambda z, y, x, c: (z, y, x + 1, 1 - c))),
        move(outs[1], pick(to_sibling, lambda z, y, x, c: (z, y, x - 1, c))),
        move(outs[3], pick(lambda z, y, x, c: (z, y, x, c), lambda z, y, x, c: (z, y, x - 1, 1 - c))),
    ]

    packed = kernel(pack_kernel, ((16, 192, 128), BF16), place, sums[own], sibling(sums[sib]), name="pack")
    parts = lax.all_to_all(packed, ("z", "y"), split_axis=0, concat_axis=0, tiled=True)
    shapes = (((2 * HALF, 256), BF16), ((8, 128), F32))
    weight_grad, done = kernel(join_kernel, shapes, *got, name="join", flops=10**11)
    query_grad = kernel(decode_kernel, ((128, 1024), BF16), parts, decoder, done, name="decode")
    return query_grad, weight_grad


def solution(mesh):
    fine = Mesh(mesh.devices.reshape(4, 4, 2, 2, 2), AXES)
    label, dp = AXES[:3], AXES[3:]
    return jax.shard_map(
        shards,
        mesh=fine,
        in_specs=(P(AXES, None), P(AXES, None), P(AXES), P(label, None), P(), P()),
        out_specs=(P(AXES, None), P(label, dp)),
        check_vma=False,
    )
```

```python
import functools
import itertools

import jax
import jax.numpy as jnp
from jax import lax
from jax.experimental import pallas as pl
from jax.experimental.pallas import tpu as pltpu
from jax.sharding import Mesh, PartitionSpec as P

AXES = ("z", "y", "xl", "xh", "core")
BF16, F32, I32 = jnp.bfloat16, jnp.float32, jnp.int32
TAIL = 16
HALF = 512
VMEM_LIMIT = 12 * 2**20
OFFSETS = (0, 3, 1, 2)


def pairs(target):
    flat = lambda z, y, x, c: (((z % 4 * 4 + y % 4) * 2 + x % 2) * 2 + x % 4 // 2) * 2 + c
    places = itertools.product(range(4), range(4), range(4), range(2))
    return [(flat(*at), flat(*target(*at))) for at in places if target(*at) is not None]


def move(array, target):
    return lax.ppermute(array, AXES, pairs(target))


def hop(phase, step):
    return lambda z, y, x, c: (z + step, y, x, c) if c == phase else (z, y + step, x, c)


def to_sibling(z, y, x, c):
    return z, y, x, 1 - c


def to_user(z, y, x, c):
    return (z, y, x ^ 1, c) if c == x % 2 else (z, y, x, 1 - c)


def low_kernel(own_ref, back_ref, low_ref):
    low_ref[:128, :] = own_ref[:128, :]
    low_ref[128:, :] = back_ref[:128, :]


def high_kernel(place, own_ref, back_ref, ahead_ref, far_ref, high_ref):
    refs = (own_ref, back_ref, ahead_ref, far_ref)
    high_ref[:128, :] = ahead_ref[:128, :]
    high_ref[128:256, :] = far_ref[:128, :]
    row = lax.broadcasted_iota(I32, (TAIL, 1024), 0)
    tail = jnp.zeros((TAIL, 1024), F32)
    for i, ref in enumerate(refs):
        ids = ref[128:144, :].astype(F32)
        for digit in range(2):
            tail = jnp.where(row == 2 * i + digit, ids[digit : digit + 1, :], tail)
    high_ref[256:, :] = tail.astype(BF16)


def encode(w_ref, enc_ref, wet_ref):
    we = lax.dot_general(
        enc_ref[...], w_ref[...], (((1,), (1,)), ((), ())), preferred_element_type=F32
    )
    high = we.astype(BF16)
    wet_ref[:192, :] = high
    wet_ref[192:, :] = (we - high.astype(F32)).astype(BF16)


def target_bits(tail, block, base):
    digits = tail[2 * block : 2 * block + 2, :]
    local = (digits[0:1] * 256 + digits[1:2]) - base
    low, bit = local & 7, jnp.left_shift(1, (local >> 3) & 31)
    words = [jnp.where((local >> 8) == w, bit, 0) for w in range(4)]
    row = lax.broadcasted_iota(I32, (8, 128), 0)
    bits = [jnp.zeros((8, 128), I32)] * 4
    for slot in range(8):
        lanes = slice(slot * 128, (slot + 1) * 128)
        here = jnp.broadcast_to(low[:, lanes], (8, 128)) == row
        for w in range(4):
            word = jnp.broadcast_to(words[w][:, lanes], (8, 128))
            bits[w] = bits[w] | jnp.where(here, word, 0)
    return bits


def quarters(x, core):
    keeps = core == lax.rem(x, 2)
    half, next_half = x // 2, lax.rem(x + 1, 4) // 2
    away = jnp.where(keeps, 1 - half, next_half)
    column = jnp.where(keeps, 1 - core, core)
    return 2 * away + column, 2 * (1 - away) + column, 2 * away + 1 - column, 2 * (1 - away) + 1 - column


def chunk_kernel(enc_at, stage, scale, *refs):
    n = len(enc_at)
    place, q_refs, refs = refs[0], refs[1 : 1 + 2 * n], refs[1 + 2 * n :]
    z, y, x, core = (place[i] for i in range(4))
    base = ((z * 4 + y) * 2 + core) * 2 * HALF
    w_ref, refs = refs[0], refs[1:]
    q_all, bits, refs = refs[-2], refs[-1], refs[:-2]
    if stage == 0:
        outs, grads = refs[:1], refs[1]
    else:
        grads, refs = refs[-1], refs[:-1]
        total_ref, wet_ref, refs = refs[0], refs[1], refs[2:]
        if stage == 3:
            refs, (narrow, out_sems) = refs[:-2], refs[-2:]
        named = sorted({out for out, _ in enc_at})
        refs = refs[len(named) :]
        encs, outs = dict(zip(named, refs)), refs[len(named) :]
    for i in range(n):
        low, high = q_refs[2 * i : 2 * i + 2]
        q_all[512 * i : 512 * i + 256, :] = low[...]
        q_all[512 * i + 256 : 512 * i + 512, :] = high[:256, :]
        tail = high[256:, :].astype(F32).astype(I32)
        for b in range(4):
            lanes = slice(512 * i + 128 * b, 512 * i + 128 * b + 128)
            for w, word in enumerate(target_bits(tail, b, base)):
                bits[w, :, lanes] = word
    group = lax.broadcasted_iota(I32, (32, 1, 1), 0)
    for i in range(2):
        rows = slice(i * HALF, (i + 1) * HALF)
        for j in range(n):
            lanes = slice(512 * j, 512 * j + 512)
            logits = lax.dot_general(
                w_ref[rows, :], q_all[lanes, :], (((1,), (1,)), ((), ())), preferred_element_type=F32
            )
            for w in range(2):
                hit = (bits[2 * i + w, :, lanes][None] >> group) & 1
                target = hit.reshape(256, 512).astype(F32)
                some = jax.nn.sigmoid(logits[w * 256 : w * 256 + 256]) - target
                grads[i * HALF + w * 256 : i * HALF + w * 256 + 256, lanes] = (some * scale).astype(BF16)
        if stage != 3:
            part = jnp.dot(grads[rows, :], q_all[...], preferred_element_type=F32)
            for c in range(4):
                columns = slice(256 * c, 256 * c + 256)
                old = total_ref[c, rows, :] if stage else 0.0
                outs[0][c, rows, :] = old + part[:, columns]
    if stage == 0:
        return
    if stage == 3:
        copies = []
        for o, c in enumerate(quarters(x, core)):
            columns = q_all[:, pl.ds(pl.multiple_of(c * 256, 256), 256)]
            whole = total_ref[c] + jnp.dot(grads[...], columns, preferred_element_type=F32)
            narrow[o] = whole.astype(BF16)
            copies.append(pltpu.make_async_copy(narrow.at[o], outs[o], out_sems.at[o]))
            copies[-1].start()
    encoded = jnp.dot(wet_ref[...], grads[...], preferred_element_type=F32)
    encoded = encoded[:192] + encoded[192:]
    for i, (out, column) in enumerate(enc_at):
        encs[out][:, column : column + 512] = encoded[:, 512 * i : 512 * i + 512]
    if stage == 3:
        for copy in copies:
            copy.wait()


def chunk(stage, place, groups, enc_at, w, scale, total=None, wet=None, sums=()):
    vmem = pl.BlockSpec(memory_space=pltpu.VMEM)
    labels, n = 2 * HALF, 512 * len(enc_at)
    named = sorted({out for out, _ in enc_at})
    args = [place, *sum(groups, []), w] + ([total, wet] if stage else [])
    at_total = len(args) - 2
    shapes, aliases = [], {}
    if stage:
        shapes = [jax.ShapeDtypeStruct((192, 2048), F32) for _ in named]
        aliases = {len(args) + i: i for i in range(len(named))}
        args += [sums[i] for i in named]
    if stage == 3:
        shapes += [pltpu.HBM((labels, 256), BF16)] * 4
    else:
        if stage:
            aliases[at_total] = len(shapes)
        shapes.append(jax.ShapeDtypeStruct((4, labels, 256), F32))
    grads = [pltpu.VMEM((labels, n), BF16)]
    if stage == 0:
        shapes.append(jax.ShapeDtypeStruct((labels, n), BF16))
        grads = []
    out_specs, scratch = [vmem] * len(shapes), []
    if stage == 3:
        out_specs[-4:] = [pl.BlockSpec(memory_space=pltpu.HBM)] * 4
        scratch = [pltpu.VMEM((4, labels, 256), BF16), pltpu.SemaphoreType.DMA((4,))]
    out = pl.pallas_call(
        functools.partial(chunk_kernel, enc_at, stage, scale),
        in_specs=[pl.BlockSpec(memory_space=pltpu.SMEM)] + [vmem] * (len(args) - 1),
        out_specs=out_specs,
        out_shape=shapes,
        scratch_shapes=[*scratch, *grads, pltpu.VMEM((n, 1024), BF16), pltpu.VMEM((4, 8, n), I32)],
        input_output_aliases=aliases,
        compiler_params=pltpu.CompilerParams(vmem_limit_bytes=VMEM_LIMIT),
        cost_estimate=pl.CostEstimate(
            flops=2 * n * labels * (2 * 1024 + 384), bytes_accessed=2**20, transcendentals=0
        ),
        name="chunk",
    )(*args)
    if stage == 0:
        return out
    new = dict(enumerate(sums)) | dict(zip(named, out))
    return ([new[0], new[1]], *out[len(named) :])


def early_kernel(w_ref, enc_ref, grads_ref, own_ref, sib_ref, wet_ref):
    encode(w_ref, enc_ref, wet_ref)
    encoded = jnp.dot(wet_ref[...], grads_ref[...], preferred_element_type=F32)
    encoded = encoded[:192] + encoded[192:]
    own_ref[:, :512] = encoded[:, :512]
    sib_ref[:, :512] = encoded[:, 512:]


def pack_kernel(place, *refs):
    own, sib, out = refs
    z, y, core = place[0], place[1], place[3]
    first, second = jnp.where(core == 0, z, y), jnp.where(core == 0, y, z)
    for part in range(4):
        for block in range(4):
            lanes = slice(512 * part + 128 * block, 512 * part + 128 * block + 128)
            j, i = lax.rem(first + OFFSETS[block], 4), lax.rem(second + OFFSETS[part], 4)
            out[jnp.where(core == 0, j * 4 + i, i * 4 + j)] = (own[:, lanes] + sib[:, lanes]).astype(BF16)


def decode_kernel(parts_ref, dec_ref, after_ref, out_ref):
    total = parts_ref[0].astype(F32)
    for i in range(1, 16):
        total += parts_ref[i].astype(F32)
    rest, result = total, None
    for _ in range(3):
        digit = rest.astype(BF16)
        rest = rest - digit.astype(F32)
        part = lax.dot_general(digit, dec_ref[...], (((0,), (0,)), ((), ())), preferred_element_type=F32)
        result = part if result is None else result + part
    out_ref[...] = result.astype(BF16)


def join_kernel(*refs):
    total = refs[0][...].astype(F32)
    for ref in refs[1:4]:
        total += ref[...].astype(F32)
    refs[4][...] = total.astype(BF16)
    refs[5][...] = jnp.zeros_like(refs[5])


def kernel(body, out, *args, name, flops=10**6):
    place = lambda a: pltpu.SMEM if a.shape == (4,) else pltpu.VMEM
    one = not isinstance(out[0][0], tuple)
    shapes = [jax.ShapeDtypeStruct(*o) for o in ([out] if one else out)]
    result = pl.pallas_call(
        body,
        in_specs=[pl.BlockSpec(memory_space=place(a)) for a in args],
        out_specs=[pl.BlockSpec(memory_space=pltpu.VMEM)] * len(shapes),
        out_shape=shapes,
        compiler_params=pltpu.CompilerParams(vmem_limit_bytes=VMEM_LIMIT),
        cost_estimate=pl.CostEstimate(flops=flops, bytes_accessed=2**10, transcendentals=0),
        name=name,
    )(*args)
    return result[0] if one else result


def after(arrays, *others):
    anywhere = pl.BlockSpec(memory_space=pl.ANY)
    n = len(arrays)
    tied = pl.pallas_call(
        lambda *refs: None,
        in_specs=[anywhere] * (n + len(others)),
        out_specs=[anywhere] * n,
        out_shape=[jax.ShapeDtypeStruct(a.shape, a.dtype) for a in arrays],
        input_output_aliases={i: i for i in range(n)},
        compiler_params=pltpu.CompilerParams(vmem_limit_bytes=2**20),
        cost_estimate=pl.CostEstimate(flops=0, bytes_accessed=0, transcendentals=0),
        name="after",
    )(*arrays, *others)
    return list(tied)


def shards(queries, label_ids, label_counts, weights, encoder, decoder):
    z, y, xl, xh, core = (lax.axis_index(a) for a in AXES)
    scale = float(queries.shape[0] * 128) ** (-0.5)

    slot = lax.broadcasted_iota(I32, (8, 128), 0)
    ids = jnp.where(slot < label_counts[None, :], label_ids.T, 255 * 256).reshape(1, 1024)
    tail = jnp.concatenate([ids >> 8, ids & 255, jnp.zeros((TAIL - 2, 1024), I32)], axis=0)
    block = jnp.concatenate([queries, tail.astype(BF16)], axis=0)

    place = jnp.stack([z, y, 2 * xh + xl, core]).astype(I32)
    w = move(weights, to_user)
    far, ahead, back = (move(block, hop(0, step)) for step in (2, -1, 1))
    low = kernel(low_kernel, ((256, 1024), BF16), block, back, name="low")
    high = kernel(high_kernel, ((256 + TAIL, 1024), BF16), place, block, back, ahead, far, name="high")
    low_back, high_ahead = move(low, hop(1, 1)), move(high, hop(1, -1))
    high_back, low_ahead = move(high, hop(1, 1)), move(low, hop(1, -1))
    sibling = lambda array: move(array, to_sibling)
    row, own, sib = [low, high], 0, 1
    rows = [row, [sibling(low), sibling(high)]]
    total, early_grads = chunk(0, place, rows, ((own, 0), (sib, 0)), w, scale)
    sums_wet = kernel(
        early_kernel,
        (((192, 2048), F32), ((192, 2048), F32), ((384, 2 * HALF), BF16)),
        w, encoder.T, early_grads, name="early", flops=2 * 1024 * 1024 * 512,
    )
    low_back, high_ahead = after([low_back, high_ahead], early_grads)
    far = [move(low_back, hop(1, 1)), move(high_ahead, hop(1, -1))]
    early = [sibling(low_back), sibling(high_ahead)]
    high_back, low_ahead = after([high_back, low_ahead], *early, sums_wet[2])
    late = [sibling(high_back), sibling(low_ahead)]
    back, ahead = [low_back, high_back], [low_ahead, high_ahead]
    sums, wet = sums_wet[:2], sums_wet[2]
    sums, total = chunk(1, place, [back, ahead], ((own, 512), (own, 1024)), w, scale, total, wet, sums)
    far = after(far, sums[own])
    back, ahead = [early[0], late[0]], [late[1], early[1]]
    sums, total = chunk(2, place, [back, ahead], ((sib, 512), (sib, 1024)), w, scale, total, wet, sums)
    far_sib = [sibling(f) for f in far]
    sums, *outs = chunk(3, place, [far, far_sib], ((own, 1536), (sib, 1536)), w, scale, total, wet, sums)

    pick = lambda same, other: lambda z, y, x, c: same(z, y, x, c) if c == x % 2 else other(z, y, x, c)
    got = [
        move(outs[0], pick(lambda z, y, x, c: (z, y, x + 2, 1 - c), lambda z, y, x, c: (z, y, x + 1, c))),
        move(outs[2], pick(lambda z, y, x, c: (z, y, x + 2, c), lambda z, y, x, c: (z, y, x + 1, 1 - c))),
        move(outs[1], pick(to_sibling, lambda z, y, x, c: (z, y, x - 1, c))),
        move(outs[3], pick(lambda z, y, x, c: (z, y, x, c), lambda z, y, x, c: (z, y, x - 1, 1 - c))),
    ]

    packed = kernel(pack_kernel, ((16, 192, 128), BF16), place, sums[own], sibling(sums[sib]), name="pack")
    parts = lax.all_to_all(packed, ("z", "y"), split_axis=0, concat_axis=0, tiled=True)
    shapes = (((2 * HALF, 256), BF16), ((8, 128), F32))
    weight_grad, done = kernel(join_kernel, shapes, *got, name="join", flops=10**11)
    query_grad = kernel(decode_kernel, ((128, 1024), BF16), parts, decoder, done, name="decode")
    return query_grad, weight_grad


def solution(mesh):
    fine = Mesh(mesh.devices.reshape(4, 4, 2, 2, 2), AXES)
    label, dp = AXES[:3], AXES[3:]
    return jax.shard_map(
        shards,
        mesh=fine,
        in_specs=(P(AXES, None), P(AXES, None), P(AXES), P(label, None), P(), P()),
        out_specs=(P(AXES, None), P(label, dp)),
        check_vma=False,
    )
```

```python
import functools
import itertools

import jax
import jax.numpy as jnp
from jax import lax
from jax.experimental import pallas as pl
from jax.experimental.pallas import tpu as pltpu
from jax.sharding import Mesh, PartitionSpec as P

AXES = ("z", "y", "xl", "xh", "core")
BF16, F32, I32 = jnp.bfloat16, jnp.float32, jnp.int32
TAIL = 16
HALF = 512
VMEM_LIMIT = 12 * 2**20
OFFSETS = (0, 3, 1, 2)


def pairs(target):
    flat = lambda z, y, x, c: (((z % 4 * 4 + y % 4) * 2 + x % 2) * 2 + x % 4 // 2) * 2 + c
    places = itertools.product(range(4), range(4), range(4), range(2))
    return [(flat(*at), flat(*target(*at))) for at in places if target(*at) is not None]


def move(array, target):
    return lax.ppermute(array, AXES, pairs(target))


def hop(phase, step):
    return lambda z, y, x, c: (z + step, y, x, c) if c == phase else (z, y + step, x, c)


def to_sibling(z, y, x, c):
    return z, y, x, 1 - c


def to_user(z, y, x, c):
    return (z, y, x ^ 1, c) if c == x % 2 else (z, y, x, 1 - c)


def low_kernel(own_ref, back_ref, low_ref):
    low_ref[:128, :] = own_ref[:128, :]
    low_ref[128:, :] = back_ref[:128, :]


def high_kernel(place, own_ref, back_ref, ahead_ref, far_ref, high_ref):
    refs = (own_ref, back_ref, ahead_ref, far_ref)
    high_ref[:128, :] = ahead_ref[:128, :]
    high_ref[128:256, :] = far_ref[:128, :]
    row = lax.broadcasted_iota(I32, (TAIL, 1024), 0)
    tail = jnp.zeros((TAIL, 1024), F32)
    for i, ref in enumerate(refs):
        ids = ref[128:144, :].astype(F32)
        for digit in range(2):
            tail = jnp.where(row == 2 * i + digit, ids[digit : digit + 1, :], tail)
    high_ref[256:, :] = tail.astype(BF16)


def encode(w_ref, enc_ref, wet_ref):
    we = lax.dot_general(
        enc_ref[...], w_ref[...], (((1,), (1,)), ((), ())), preferred_element_type=F32
    )
    high = we.astype(BF16)
    wet_ref[:192, :] = high
    wet_ref[192:, :] = (we - high.astype(F32)).astype(BF16)


def target_bits(tail, block, base):
    digits = tail[2 * block : 2 * block + 2, :]
    local = (digits[0:1] * 256 + digits[1:2]) - base
    low, bit = local & 7, jnp.left_shift(1, (local >> 3) & 31)
    words = [jnp.where((local >> 8) == w, bit, 0) for w in range(4)]
    row = lax.broadcasted_iota(I32, (8, 128), 0)
    bits = [jnp.zeros((8, 128), I32)] * 4
    for slot in range(8):
        lanes = slice(slot * 128, (slot + 1) * 128)
        here = jnp.broadcast_to(low[:, lanes], (8, 128)) == row
        for w in range(4):
            word = jnp.broadcast_to(words[w][:, lanes], (8, 128))
            bits[w] = bits[w] | jnp.where(here, word, 0)
    return bits


def quarters(x, core):
    keeps = core == lax.rem(x, 2)
    half, next_half = x // 2, lax.rem(x + 1, 4) // 2
    away = jnp.where(keeps, 1 - half, next_half)
    column = jnp.where(keeps, 1 - core, core)
    return 2 * away + column, 2 * (1 - away) + column, 2 * away + 1 - column, 2 * (1 - away) + 1 - column


def chunk_kernel(enc_at, stage, scale, *refs):
    n = len(enc_at)
    place, q_refs, refs = refs[0], refs[1 : 1 + 2 * n], refs[1 + 2 * n :]
    z, y, x, core = (place[i] for i in range(4))
    base = ((z * 4 + y) * 2 + core) * 2 * HALF
    w_ref, refs = refs[0], refs[1:]
    q_all, bits, refs = refs[-2], refs[-1], refs[:-2]
    if stage == 0:
        outs, grads = refs[:1], refs[1]
    else:
        grads, refs = refs[-1], refs[:-1]
        total_ref, wet_ref, refs = refs[0], refs[1], refs[2:]
        if stage == 3:
            refs, (narrow, out_sems) = refs[:-2], refs[-2:]
        named = sorted({out for out, _ in enc_at})
        refs = refs[len(named) :]
        encs, outs = dict(zip(named, refs)), refs[len(named) :]
    for i in range(n):
        low, high = q_refs[2 * i : 2 * i + 2]
        q_all[512 * i : 512 * i + 256, :] = low[...]
        q_all[512 * i + 256 : 512 * i + 512, :] = high[:256, :]
        tail = high[256:, :].astype(F32).astype(I32)
        for b in range(4):
            lanes = slice(512 * i + 128 * b, 512 * i + 128 * b + 128)
            for w, word in enumerate(target_bits(tail, b, base)):
                bits[w, :, lanes] = word
    group = lax.broadcasted_iota(I32, (32, 1, 1), 0)
    for i in range(2):
        rows = slice(i * HALF, (i + 1) * HALF)
        for j in range(n):
            lanes = slice(512 * j, 512 * j + 512)
            logits = lax.dot_general(
                w_ref[rows, :], q_all[lanes, :], (((1,), (1,)), ((), ())), preferred_element_type=F32
            )
            for w in range(2):
                hit = (bits[2 * i + w, :, lanes][None] >> group) & 1
                target = hit.reshape(256, 512).astype(F32)
                some = jax.nn.sigmoid(logits[w * 256 : w * 256 + 256]) - target
                grads[i * HALF + w * 256 : i * HALF + w * 256 + 256, lanes] = (some * scale).astype(BF16)
        if stage != 3:
            part = jnp.dot(grads[rows, :], q_all[...], preferred_element_type=F32)
            for c in range(4):
                columns = slice(256 * c, 256 * c + 256)
                old = total_ref[c, rows, :] if stage else 0.0
                outs[0][c, rows, :] = old + part[:, columns]
    if stage == 0:
        return
    if stage == 3:
        copies = []
        for o, c in enumerate(quarters(x, core)):
            columns = q_all[:, pl.ds(pl.multiple_of(c * 256, 256), 256)]
            whole = total_ref[c] + jnp.dot(grads[...], columns, preferred_element_type=F32)
            narrow[o] = whole.astype(BF16)
            copies.append(pltpu.make_async_copy(narrow.at[o], outs[o], out_sems.at[o]))
            copies[-1].start()
    encoded = jnp.dot(wet_ref[...], grads[...], preferred_element_type=F32)
    encoded = encoded[:192] + encoded[192:]
    for i, (out, column) in enumerate(enc_at):
        encs[out][:, column : column + 512] = encoded[:, 512 * i : 512 * i + 512]
    if stage == 3:
        for copy in copies:
            copy.wait()


def chunk(stage, place, groups, enc_at, w, scale, total=None, wet=None, sums=()):
    vmem = pl.BlockSpec(memory_space=pltpu.VMEM)
    labels, n = 2 * HALF, 512 * len(enc_at)
    named = sorted({out for out, _ in enc_at})
    args = [place, *sum(groups, []), w] + ([total, wet] if stage else [])
    at_total = len(args) - 2
    shapes, aliases = [], {}
    if stage:
        shapes = [jax.ShapeDtypeStruct((192, 2048), F32) for _ in named]
        aliases = {len(args) + i: i for i in range(len(named))}
        args += [sums[i] for i in named]
    if stage == 3:
        shapes += [pltpu.HBM((labels, 256), BF16)] * 4
    else:
        if stage:
            aliases[at_total] = len(shapes)
        shapes.append(jax.ShapeDtypeStruct((4, labels, 256), F32))
    grads = [pltpu.VMEM((labels, n), BF16)]
    if stage == 0:
        shapes.append(jax.ShapeDtypeStruct((labels, n), BF16))
        grads = []
    out_specs, scratch = [vmem] * len(shapes), []
    if stage == 3:
        out_specs[-4:] = [pl.BlockSpec(memory_space=pltpu.HBM)] * 4
        scratch = [pltpu.VMEM((4, labels, 256), BF16), pltpu.SemaphoreType.DMA((4,))]
    out = pl.pallas_call(
        functools.partial(chunk_kernel, enc_at, stage, scale),
        in_specs=[pl.BlockSpec(memory_space=pltpu.SMEM)] + [vmem] * (len(args) - 1),
        out_specs=out_specs,
        out_shape=shapes,
        scratch_shapes=[*scratch, *grads, pltpu.VMEM((n, 1024), BF16), pltpu.VMEM((4, 8, n), I32)],
        input_output_aliases=aliases,
        compiler_params=pltpu.CompilerParams(vmem_limit_bytes=VMEM_LIMIT),
        cost_estimate=pl.CostEstimate(
            flops=2 * n * labels * (2 * 1024 + 384), bytes_accessed=2**20, transcendentals=0
        ),
        name="chunk",
    )(*args)
    if stage == 0:
        return out
    new = dict(enumerate(sums)) | dict(zip(named, out))
    return ([new[0], new[1]], *out[len(named) :])


def early_kernel(w_ref, enc_ref, grads_ref, own_ref, sib_ref, wet_ref):
    encode(w_ref, enc_ref, wet_ref)
    encoded = jnp.dot(wet_ref[...], grads_ref[...], preferred_element_type=F32)
    encoded = encoded[:192] + encoded[192:]
    own_ref[:, :512] = encoded[:, :512]
    sib_ref[:, :512] = encoded[:, 512:]


def pack_kernel(place, *refs):
    own, sib, out = refs
    z, y, core = place[0], place[1], place[3]
    first, second = jnp.where(core == 0, z, y), jnp.where(core == 0, y, z)
    for part in range(4):
        for block in range(4):
            lanes = slice(512 * part + 128 * block, 512 * part + 128 * block + 128)
            j, i = lax.rem(first + OFFSETS[block], 4), lax.rem(second + OFFSETS[part], 4)
            out[jnp.where(core == 0, j * 4 + i, i * 4 + j)] = (own[:, lanes] + sib[:, lanes]).astype(BF16)


def decode_kernel(parts_ref, dec_ref, after_ref, out_ref):
    total = parts_ref[0].astype(F32)
    for i in range(1, 16):
        total += parts_ref[i].astype(F32)
    rest, result = total, None
    for _ in range(3):
        digit = rest.astype(BF16)
        rest = rest - digit.astype(F32)
        part = lax.dot_general(digit, dec_ref[...], (((0,), (0,)), ((), ())), preferred_element_type=F32)
        result = part if result is None else result + part
    out_ref[...] = result.astype(BF16)


def join_kernel(*refs):
    total = refs[0][...].astype(F32)
    for ref in refs[1:4]:
        total += ref[...].astype(F32)
    refs[4][...] = total.astype(BF16)
    refs[5][...] = jnp.zeros_like(refs[5])


def kernel(body, out, *args, name, flops=10**6):
    place = lambda a: pltpu.SMEM if a.shape == (4,) else pltpu.VMEM
    one = not isinstance(out[0][0], tuple)
    shapes = [jax.ShapeDtypeStruct(*o) for o in ([out] if one else out)]
    result = pl.pallas_call(
        body,
        in_specs=[pl.BlockSpec(memory_space=place(a)) for a in args],
        out_specs=[pl.BlockSpec(memory_space=pltpu.VMEM)] * len(shapes),
        out_shape=shapes,
        compiler_params=pltpu.CompilerParams(vmem_limit_bytes=VMEM_LIMIT),
        cost_estimate=pl.CostEstimate(flops=flops, bytes_accessed=2**10, transcendentals=0),
        name=name,
    )(*args)
    return result[0] if one else result


def after(arrays, *others):
    anywhere = pl.BlockSpec(memory_space=pl.ANY)
    n = len(arrays)
    tied = pl.pallas_call(
        lambda *refs: None,
        in_specs=[anywhere] * (n + len(others)),
        out_specs=[anywhere] * n,
        out_shape=[jax.ShapeDtypeStruct(a.shape, a.dtype) for a in arrays],
        input_output_aliases={i: i for i in range(n)},
        compiler_params=pltpu.CompilerParams(vmem_limit_bytes=2**20),
        cost_estimate=pl.CostEstimate(flops=0, bytes_accessed=0, transcendentals=0),
        name="after",
    )(*arrays, *others)
    return list(tied)


def shards(queries, label_ids, label_counts, weights, encoder, decoder):
    z, y, xl, xh, core = (lax.axis_index(a) for a in AXES)
    scale = float(queries.shape[0] * 128) ** (-0.5)

    slot = lax.broadcasted_iota(I32, (8, 128), 0)
    ids = jnp.where(slot < label_counts[None, :], label_ids.T, 255 * 256).reshape(1, 1024)
    tail = jnp.concatenate([ids >> 8, ids & 255, jnp.zeros((TAIL - 2, 1024), I32)], axis=0)
    block = jnp.concatenate([queries, tail.astype(BF16)], axis=0)

    place = jnp.stack([z, y, 2 * xh + xl, core]).astype(I32)
    w = move(weights, to_user)
    far, ahead, back = (move(block, hop(0, step)) for step in (2, -1, 1))
    low = kernel(low_kernel, ((256, 1024), BF16), block, back, name="low")
    low_sib = move(low, to_sibling)
    ahead, far = after([ahead, far], low_sib)
    high = kernel(high_kernel, ((256 + TAIL, 1024), BF16), place, block, back, ahead, far, name="high")
    low_back, high_ahead = move(low, hop(1, 1)), move(high, hop(1, -1))
    high_back, low_ahead = move(high, hop(1, 1)), move(low, hop(1, -1))
    sibling = lambda array: move(array, to_sibling)
    row, own, sib = [low, high], 0, 1
    rows = [row, [low_sib, sibling(high)]]
    total, early_grads = chunk(0, place, rows, ((own, 0), (sib, 0)), w, scale)
    sums_wet = kernel(
        early_kernel,
        (((192, 2048), F32), ((192, 2048), F32), ((384, 2 * HALF), BF16)),
        w, encoder.T, early_grads, name="early", flops=2 * 1024 * 1024 * 512,
    )
    low_back, high_ahead = after([low_back, high_ahead], early_grads)
    far = [move(low_back, hop(1, 1)), move(high_ahead, hop(1, -1))]
    early = [sibling(low_back), sibling(high_ahead)]
    high_back, low_ahead = after([high_back, low_ahead], *early, sums_wet[2])
    late = [sibling(high_back), sibling(low_ahead)]
    back, ahead = [low_back, high_back], [low_ahead, high_ahead]
    sums, wet = sums_wet[:2], sums_wet[2]
    sums, total = chunk(1, place, [back, ahead], ((own, 512), (own, 1024)), w, scale, total, wet, sums)
    far = after(far, sums[own])
    back, ahead = [early[0], late[0]], [late[1], early[1]]
    sums, total = chunk(2, place, [back, ahead], ((sib, 512), (sib, 1024)), w, scale, total, wet, sums)
    far_sib = [sibling(f) for f in far]
    sums, *outs = chunk(3, place, [far, far_sib], ((own, 1536), (sib, 1536)), w, scale, total, wet, sums)

    pick = lambda same, other: lambda z, y, x, c: same(z, y, x, c) if c == x % 2 else other(z, y, x, c)
    got = [
        move(outs[0], pick(lambda z, y, x, c: (z, y, x + 2, 1 - c), lambda z, y, x, c: (z, y, x + 1, c))),
        move(outs[2], pick(lambda z, y, x, c: (z, y, x + 2, c), lambda z, y, x, c: (z, y, x + 1, 1 - c))),
        move(outs[1], pick(to_sibling, lambda z, y, x, c: (z, y, x - 1, c))),
        move(outs[3], pick(lambda z, y, x, c: (z, y, x, c), lambda z, y, x, c: (z, y, x - 1, 1 - c))),
    ]

    packed = kernel(pack_kernel, ((16, 192, 128), BF16), place, sums[own], sibling(sums[sib]), name="pack")
    parts = lax.all_to_all(packed, ("z", "y"), split_axis=0, concat_axis=0, tiled=True)
    shapes = (((2 * HALF, 256), BF16), ((8, 128), F32))
    weight_grad, done = kernel(join_kernel, shapes, *got, name="join", flops=10**11)
    query_grad = kernel(decode_kernel, ((128, 1024), BF16), parts, decoder, done, name="decode")
    return query_grad, weight_grad


def solution(mesh):
    fine = Mesh(mesh.devices.reshape(4, 4, 2, 2, 2), AXES)
    label, dp = AXES[:3], AXES[3:]
    return jax.shard_map(
        shards,
        mesh=fine,
        in_specs=(P(AXES, None), P(AXES, None), P(AXES), P(label, None), P(), P()),
        out_specs=(P(AXES, None), P(label, dp)),
        check_vma=False,
    )
```
